128 devices in a mesh: row: 4 (over x_hi, core), reader: 32 (over x_lo, z, y).
Axes of the slice: x: 4 (x_hi: 2, x_lo: 2; x = x_hi * 2 + x_lo), y: 4, z: 4, core: 2. Of those that a mesh axis runs over, the one named last changes fastest.
Arguments:
- records: bfloat16 [4, 32, 256, 4096], P('row', None, 'reader'), may hold values from -6 to 6
- lengths: int32 [4, 32], replicated, may hold values from 1 to 256, as said below
- assignment: int32 [4, 32], replicated, may hold values from 0 to 31, as said below
- segment_ids: int32 [4, 32, 256], replicated, may hold values from 0 to 11, never falling along the last dimension, each value on 1 to 64 neighbouring positions
- norm_gain: float32 [4096], replicated, may hold values from 0.6 to 6
- w_qkv: bfloat16 [4096, 4, 1280], P('reader', 'row'), may hold values from -0.09375 to 0.09375
- w_out: bfloat16 [4096, 4, 1024], P('reader', 'row'), may hold values from -0.09375 to 0.09375
- score_weights: float32 [4096], replicated, may hold values from -0.09375 to 0.09375
Outputs:
- hidden_out: bfloat16 [28672, 4096], P('reader', 'row')
- record_scores: float32 [32, 4], P('reader')
The draws below stay inside these ranges and needn't reach their ends.
Inputs may be any that keep to these rules, and one draw needn't show every extreme that they name: `assignment`: each row names every scorer shard exactly once. For every scorer shard the lengths of the records that name it, one from each row, sum to 896; some record has 256. `segment_ids`: along a record the document numbers never fall.
All inputs are finite; a program needn't handle non-finite values.
Results may differ from the reference program's by a relative error of at most 0.015.
The reference program's roundings to bfloat16 on the way count: a program that leaves them out, or rounds other values in their place, can miss the bound.
Values may be sent and summed in bfloat16 or wider, within the bound.
No kernel may reach another device: no remote copies, remote signals or barrier semaphores. Data moves between devices by JAX's collectives and lax.ppermute only.
A program may use at most 128 MiB of HBM per device.

```python
import math
import jax
import jax.numpy as jnp
import numpy as np
from jax import lax

D = 4096
HS = 128
KVH = 4
GROUP = 8
RECLEN = 256
TOK_DEV = 896
RECS = 32
N_ROW = 4
N_READER = 32


def record_plan(key):
    base = jax.random.fold_in(key, 4711)
    key_cut, key_full, key_roll, key_perm = jax.random.split(base, 4)
    deficit = RECLEN // 2
    cuts = jax.random.randint(key_cut, (N_READER, N_ROW - 1), 0, deficit + 1).astype(jnp.int32)
    full_scorer = jax.random.randint(key_full, (), 0, N_READER).astype(jnp.int32)
    scorer_ids = jnp.arange(N_READER, dtype=jnp.int32)
    first_col = (jnp.arange(N_ROW - 1, dtype=jnp.int32) == 0)[None, :]
    cuts = jnp.where((scorer_ids[:, None] == full_scorer) & first_col, 0, cuts).astype(jnp.int32)
    cuts = jnp.sort(cuts, axis=1)
    edges = jnp.concatenate([jnp.zeros((N_READER, 1), jnp.int32), cuts, jnp.full((N_READER, 1), deficit, jnp.int32)], axis=1)
    shortfall = (edges[:, 1:] - edges[:, :-1]).astype(jnp.int32)
    shifts = jax.random.randint(key_roll, (N_READER,), 0, N_ROW).astype(jnp.int32)
    slots = jnp.arange(N_ROW, dtype=jnp.int32)[None, :]
    rolled = ((slots + shifts[:, None]) % N_ROW).astype(jnp.int32)
    shortfall = jnp.take_along_axis(shortfall, rolled, axis=1)
    per_scorer = (RECLEN - shortfall).astype(jnp.int32)
    orders = jax.vmap(lambda one_key: jax.random.permutation(one_key, N_READER))(jax.random.split(key_perm, N_ROW)).astype(jnp.int32)
    row_ids = jnp.arange(N_ROW, dtype=jnp.int32)[:, None]
    record_lens = per_scorer[orders, row_ids]
    return (record_lens.astype(jnp.int32), orders)


def draw_lengths(key, part):
    return record_plan(key)[0]


def draw_assignment(key, part):
    return record_plan(key)[1]


def draw_norm_gain(key, part):
    values = jax.random.uniform(jax.random.fold_in(key, 31), (D,), jnp.float32, 0.6, 1.4)
    return values.astype(jnp.float32)


def shard_levels(rng, shape, cuts, low, top_value):
    loudness, own = 1.0, jax.random.fold_in(rng, 6)
    for position, parts in cuts:
        steps = jnp.exp(jax.random.uniform(jax.random.fold_in(own, position), (parts,), jnp.float32, low / len(cuts), top_value / len(cuts)))
        loudness = loudness * jnp.repeat(steps, shape[position] // parts).reshape([-1 if axis == position else 1 for axis in range(len(shape))])
    return loudness


def length_profile(number_of, total, limit, slope):
    loads = [(1 << 20) // math.isqrt(rank ** slope) + 1 for rank in range(2, number_of + 1)]
    surplus, holding = total - limit - (number_of - 1), [1] * (number_of - 1)
    while surplus > 0:
        candidates = [i for i in range(number_of - 1) if holding[i] < limit]
        whole, budget = sum([loads[i] for i in candidates]), surplus
        for i in candidates:
            extra = min(limit - holding[i], max(1, budget * loads[i] // whole), surplus)
            holding[i] = holding[i] + extra
            surplus = surplus - extra
    return np.array([limit] + holding)


def uneven_parts(key, amount, total, most, lean):
    if amount == 2:
        one = jax.random.randint(key, (), max(1, total - most), min(most, total - 1) + 1)
        return jnp.stack([one, total - one])
    sizes = jnp.asarray(length_profile(amount, total, most, lean), jnp.int32)
    twos = (amount - 1) // 2
    source_of, receiver = sizes[1:1 + 2 * twos:2], sizes[2:2 + 2 * twos:2]
    margin = jnp.minimum(source_of - 1, most - receiver)
    moved = jax.random.randint(jax.random.fold_in(key, 1), (twos,), 0, 1 << 20) % (margin + 1)
    sizes = sizes.at[1:1 + 2 * twos:2].set(source_of - moved).at[2:2 + 2 * twos:2].set(receiver + moved)
    return sizes[jax.random.permutation(jax.random.fold_in(key, 2), amount)]


def normal_values(rng, shape, deviation, limit, cuts=(), held_as=jnp.bfloat16):
    gain = shard_levels(rng, shape, cuts, -0.22, 0.18) if cuts else 1.0
    entries = jax.random.normal(rng, shape, jnp.float32) * deviation * gain
    return jnp.minimum(jnp.maximum(entries, -limit), limit).astype(held_as)


def setup_inputs(seed: int = 0) -> dict:
    key_of = jax.random.split(jax.random.key(seed), 9)
    return {
        "records": normal_values(key_of[0], (N_ROW, RECS, RECLEN, D), 1.0, 6.0, ((0, 4), (2, 32))),
        "lengths": draw_lengths(jax.random.fold_in(key_of[8], 71), 0),
        "assignment": draw_assignment(jax.random.fold_in(key_of[8], 71), 0),
        "segment_ids": jax.vmap(lambda own: jnp.searchsorted(jnp.cumsum(uneven_parts(own, 12, RECLEN, RECLEN // 4, 2)), jnp.arange(RECLEN), side="right"))(jax.random.split(key_of[3], N_ROW * RECS)).reshape((N_ROW, RECS, RECLEN)).astype(jnp.int32),
        "norm_gain": draw_norm_gain(jax.random.fold_in(key_of[8], 71), 0),
        "w_qkv": normal_values(key_of[5], (D, KVH, (GROUP + 2) * HS), D ** -0.5, 0.09375, ((0, 32), (1, 4))),
        "w_out": normal_values(key_of[6], (D, KVH, GROUP * HS), (KVH * GROUP * HS) ** -0.5, 0.09375, ((0, 32), (1, 4))),
        "score_weights": normal_values(key_of[7], (D,), D ** -0.5, 0.09375, (), jnp.float32),
    }


ROPE_BASE = 500000.0

def rotary(values, cosine, sine):
    half = values.shape[-1] // 2
    shape = (values.shape[0],) + (1,) * (values.ndim - 2) + (half,)
    cosine = cosine.reshape(shape)
    sine = sine.reshape(shape)
    first = values[..., :half]
    second = values[..., half:]
    return jnp.concatenate([first * cosine - second * sine, second * cosine + first * sine], axis=-1)

def masked_softmax(logits, allowed):
    held = jnp.where(allowed, logits, -1e+30)
    top = lax.optimization_barrier(jnp.max(held, axis=-1, keepdims=True))
    weights = jnp.where(allowed, jnp.exp(held - top), 0.0)
    return weights / lax.optimization_barrier(jnp.sum(weights, axis=-1, keepdims=True))

def pack_plan(lengths, assignment, scorer):
    rows = jnp.arange(N_ROW, dtype=jnp.int32)
    chosen = jnp.argmax(assignment == scorer, axis=1).astype(jnp.int32)
    record_lens = jnp.take_along_axis(lengths, chosen[:, None], axis=1)[:, 0].astype(jnp.int32)
    ends = jnp.cumsum(record_lens).astype(jnp.int32)
    starts = ends - record_lens
    place = jnp.arange(TOK_DEV, dtype=jnp.int32)
    owner = lax.optimization_barrier(jnp.sum((place[:, None] >= ends[None, :-1]).astype(jnp.int32), axis=1)).astype(jnp.int32)
    matches = owner[:, None] == rows[None, :]
    within = (place - lax.optimization_barrier(jnp.sum(jnp.where(matches, starts[None, :], 0), axis=1))).astype(jnp.int32)
    picked = lax.optimization_barrier(jnp.sum(jnp.where(matches, chosen[None, :], 0), axis=1)).astype(jnp.int32)
    return (record_lens, owner, within, picked, matches)

def reference(records, lengths, assignment, segment_ids, norm_gain, w_qkv, w_out, score_weights):
    inv_freq = ROPE_BASE ** (-(jnp.arange(HS // 2, dtype=jnp.float32) * 2.0 / HS))
    heads_row = KVH // N_ROW

    def score_one(scorer):
        record_lens, owner, within, picked, matches = pack_plan(lengths, assignment, scorer)
        packed = records[owner, picked, within]
        segs = segment_ids[owner, picked, within]
        packed_f = packed.astype(jnp.float32)
        scale = lax.rsqrt(lax.optimization_barrier(jnp.mean(packed_f * packed_f, axis=1, keepdims=True)) + 1e-05)
        normed = (packed_f * scale * norm_gain).astype(jnp.bfloat16)
        projected = jnp.dot(normed, w_qkv.reshape(D, -1), preferred_element_type=jnp.float32)
        projected = projected.reshape(TOK_DEV, KVH, GROUP + 2, HS)
        angle = within.astype(jnp.float32)[:, None] * inv_freq[None, :]
        cosine = jnp.cos(angle)
        sine = jnp.sin(angle)
        queries = rotary(projected[:, :, :GROUP], cosine, sine).astype(jnp.bfloat16)
        keys = rotary(projected[:, :, GROUP], cosine, sine).astype(jnp.bfloat16)
        values = projected[:, :, GROUP + 1].astype(jnp.bfloat16)
        place = jnp.arange(TOK_DEV, dtype=jnp.int32)
        allowed = (owner[:, None] == owner[None, :]) & (segs[:, None] == segs[None, :]) & (place[None, :] <= place[:, None])
        logits = jnp.einsum('qhgd,khd->hgqk', queries.astype(jnp.float32), keys.astype(jnp.float32)) * (1.0 / math.sqrt(HS))
        probs = masked_softmax(logits, allowed[None, None]).astype(jnp.bfloat16)
        mixed = jnp.einsum('hgqk,khd->qhgd', probs.astype(jnp.float32), values.astype(jnp.float32)).astype(jnp.bfloat16)
        total = packed_f
        for row in range(N_ROW):
            part = mixed[:, row * heads_row:(row + 1) * heads_row].reshape(TOK_DEV, -1)
            weights = w_out[:, row * heads_row:(row + 1) * heads_row].reshape(D, -1)
            partial_value = jnp.dot(part, weights.T, preferred_element_type=jnp.float32).astype(jnp.bfloat16)
            partial_value = lax.optimization_barrier(partial_value)
            total = total + partial_value.astype(jnp.float32)
        hidden = total.astype(jnp.bfloat16)
        token_scores = jnp.dot(total, score_weights, precision=lax.Precision.HIGHEST)
        record_sums = jnp.dot(token_scores, matches.astype(jnp.float32), precision=lax.Precision.HIGHEST)
        return (hidden, record_sums / record_lens.astype(jnp.float32))
    hidden, scores = lax.map(score_one, jnp.arange(N_READER, dtype=jnp.int32))
    return (hidden.reshape(N_READER * TOK_DEV, D), scores)
```

```python
import math

import jax
import jax.numpy as jnp
from jax import lax
from jax.experimental import pallas as pl
from jax.experimental.pallas import tpu as pltpu
from jax.sharding import Mesh, PartitionSpec as P

HS = 128
GROUP = 8
RECLEN = 256
WIDTH = 4096
TOK = 896
QKV = (GROUP + 2) * HS
HEADS = GROUP * HS
COLS = WIDTH // 4
ROPE_BASE = 500000.0
BLK = 128
VMEM_LIMIT = 56 * 1024 * 1024

CORE_ZY = ("co", "z", "y")


def ring(axis, size, step):
    return lambda v: lax.ppermute(v, axis, [(i, (i + step) % size) for i in range(size)])


def plane_perm(step, first):
    pairs = []
    for co in range(2):
        for z in range(4):
            for y in range(4):
                along_y = (co == 0) == first
                z2, y2 = (z, (y + step) % 4) if along_y else ((z + step) % 4, y)
                pairs.append((co * 16 + z * 4 + y, co * 16 + z2 * 4 + y2))
    return lambda v: lax.ppermute(v, CORE_ZY, pairs)


def plane_gather_first(block):
    one = plane_perm(1, True)(block)
    three = plane_perm(-1, True)(block)
    two = plane_perm(2, True)(block)
    return jnp.concatenate([block, one, two, three], axis=0)


def plane_gather_second(line):
    half = line.shape[0] // 2
    one = plane_perm(1, False)(line)
    three = plane_perm(-1, False)(line)
    two_a = plane_perm(1, False)(one[:half])
    two_b = plane_perm(-1, False)(three[half:])
    return [line, one, three, two_a, two_b]


def piece_of(a, b, rows):
    if b == 0:
        return 0, a * rows
    if b == 1:
        return 1, a * rows
    if b == 3:
        return 2, a * rows
    return (3, a * rows) if a < 2 else (4, (a - 2) * rows)


def order_kernel(outgoing_ref, records_ref, out_ref, sems):
    copies = [
        pltpu.make_async_copy(records_ref.at[outgoing_ref[j]], out_ref.at[j], sems.at[j])
        for j in range(32)
    ]
    for copy in copies:
        copy.start()
    for copy in copies:
        copy.wait()


def order_records(outgoing, records):
    return pl.pallas_call(
        order_kernel,
        out_shape=jax.ShapeDtypeStruct(records.shape, records.dtype),
        in_specs=[
            pl.BlockSpec(memory_space=pltpu.SMEM),
            pl.BlockSpec(memory_space=pl.ANY),
        ],
        out_specs=pl.BlockSpec(memory_space=pl.ANY),
        scratch_shapes=[pltpu.SemaphoreType.DMA((32,))],
        cost_estimate=pl.CostEstimate(flops=0, bytes_accessed=4 << 20, transcendentals=0),
        name="order_records",
    )(outgoing, records)


def attend_kernel(
    offs_ref, xa_ref, xb_ref, gain_ref, cos_ref, sin_ref, segq_ref, segk_ref, *rest
):
    pieces = rest[:10]
    out_ref, w_ref, normed_ref, proj_ref, sems = rest[10:]
    copies = []
    for side in range(2):
        for a in range(4):
            for b in range(4):
                which, row = piece_of(a, b, BLK)
                n = side * 16 + a * 4 + b
                dst = pl.multiple_of(offs_ref[n], BLK)
                copies.append(
                    pltpu.make_async_copy(
                        pieces[side * 5 + which].at[pl.ds(row, BLK)],
                        w_ref.at[pl.ds(dst, BLK)],
                        sems.at[n],
                    )
                )
    for copy in copies:
        copy.start()
    gain = gain_ref[...]
    for part, x_ref in enumerate((xa_ref, xb_ref)):

        @pl.loop(0, RECLEN // 16)
        def _(i, part=part, x_ref=x_ref):
            row = pl.multiple_of(i * 16, 16)
            x = x_ref[pl.ds(row, 16), :].astype(jnp.float32)
            scale = lax.rsqrt(jnp.mean(x * x, axis=1, keepdims=True) + 1e-05)
            out_row = pl.multiple_of(part * RECLEN + i * 16, 16)
            normed_ref[pl.ds(out_row, 16), :] = (x * scale * gain).astype(jnp.bfloat16)

    for copy in copies:
        copy.wait()

    @pl.loop(0, QKV // 256)
    def _(n):
        col = pl.multiple_of(n * 256, 256)
        proj_ref[:, pl.ds(col, 256)] = jnp.dot(
            normed_ref[...], w_ref[:, pl.ds(col, 256)], preferred_element_type=jnp.float32
        )

    cosine = cos_ref[...]
    sine = sin_ref[...]
    place_q = lax.broadcasted_iota(jnp.int32, (RECLEN, RECLEN), 0)
    place_k = lax.broadcasted_iota(jnp.int32, (RECLEN, RECLEN), 1)
    scaling = 1.0 / math.sqrt(HS)
    for part in range(2):
        rows = pl.ds(part * RECLEN, RECLEN)
        allowed = (segq_ref[part] == segk_ref[part]) & (place_k <= place_q)
        key = proj_ref[rows, GROUP * HS : (GROUP + 1) * HS]
        key = (key * cosine + pltpu.roll(key, HS // 2, 1) * sine).astype(jnp.bfloat16)
        value = proj_ref[rows, (GROUP + 1) * HS : (GROUP + 2) * HS].astype(jnp.bfloat16)

        @pl.loop(0, GROUP)
        def _(g, rows=rows, allowed=allowed, key=key, value=value):
            col = pl.multiple_of(g * HS, HS)
            query = proj_ref[rows, pl.ds(col, HS)]
            query = (query * cosine + pltpu.roll(query, HS // 2, 1) * sine).astype(jnp.bfloat16)
            logits = (
                lax.dot_general(
                    query, key, (((1,), (1,)), ((), ())), preferred_element_type=jnp.float32
                )
                * scaling
            )
            held = jnp.where(allowed, logits, -1e30)
            top = jnp.max(held, axis=-1, keepdims=True)
            weights = jnp.where(allowed, jnp.exp(held - top), 0.0)
            probs = (weights / jnp.sum(weights, axis=-1, keepdims=True)).astype(jnp.bfloat16)
            out_ref[rows, pl.ds(col, HS)] = jnp.dot(
                probs, value, preferred_element_type=jnp.float32
            ).astype(jnp.bfloat16)


def attend(offs, xa, xb, gain, cosine, sine, segq, segk, pieces):
    vmem = pl.BlockSpec(memory_space=pltpu.VMEM)
    return pl.pallas_call(
        attend_kernel,
        out_shape=jax.ShapeDtypeStruct((2 * RECLEN, HEADS), jnp.bfloat16),
        in_specs=[pl.BlockSpec(memory_space=pltpu.SMEM)]
        + [vmem] * 7
        + [pl.BlockSpec(memory_space=pl.ANY)] * 10,
        out_specs=vmem,
        scratch_shapes=[
            pltpu.VMEM((WIDTH, QKV), jnp.bfloat16),
            pltpu.VMEM((2 * RECLEN, WIDTH), jnp.bfloat16),
            pltpu.VMEM((2 * RECLEN, QKV), jnp.float32),
            pltpu.SemaphoreType.DMA((32,)),
        ],
        compiler_params=pltpu.CompilerParams(vmem_limit_bytes=VMEM_LIMIT),
        cost_estimate=pl.CostEstimate(
            flops=2 * 512 * WIDTH * QKV, bytes_accessed=32 << 20, transcendentals=1 << 20
        ),
        name="attend",
    )(offs, xa, xb, gain, cosine, sine, segq, segk, *pieces)


def project_kernel(head, offs_ref, mixed_ref, *rest):
    pieces = rest[:5]
    away_ref, kept_ref, w_ref, sems = rest[5:]
    copies = []
    for a in range(4):
        for b in range(4):
            which, row = piece_of(a, b, 2 * BLK)
            n = a * 4 + b
            dst = pl.multiple_of(offs_ref[n], BLK)
            copies.append(
                pltpu.make_async_copy(
                    pieces[which].at[pl.ds(row + head * BLK, BLK)],
                    w_ref.at[pl.ds(dst, BLK)],
                    sems.at[n],
                )
            )
    for copy in copies:
        copy.start()
    for copy in copies:
        copy.wait()
    for part, out_ref in enumerate((away_ref, kept_ref)):

        @pl.loop(0, COLS // 256)
        def _(n, part=part, out_ref=out_ref):
            row = pl.multiple_of(part * COLS + n * 256, 256)
            col = pl.multiple_of(n * 256, 256)
            out_ref[:, pl.ds(col, 256)] = lax.dot_general(
                mixed_ref[...],
                w_ref[pl.ds(row, 256), :],
                (((1,), (1,)), ((), ())),
                preferred_element_type=jnp.float32,
            ).astype(jnp.bfloat16)


def project(offs, mixed, pieces, head):
    vmem = pl.BlockSpec(memory_space=pltpu.VMEM)
    tokens = mixed.shape[0]
    return pl.pallas_call(
        lambda *refs: project_kernel(head, *refs),
        out_shape=[jax.ShapeDtypeStruct((tokens, COLS), jnp.bfloat16)] * 2,
        in_specs=[pl.BlockSpec(memory_space=pltpu.SMEM), vmem]
        + [pl.BlockSpec(memory_space=pl.ANY)] * 5,
        out_specs=[vmem, vmem],
        scratch_shapes=[
            pltpu.VMEM((2 * COLS, HEADS), jnp.bfloat16),
            pltpu.SemaphoreType.DMA((16,)),
        ],
        compiler_params=pltpu.CompilerParams(vmem_limit_bytes=VMEM_LIMIT),
        cost_estimate=pl.CostEstimate(
            flops=2 * tokens * HEADS * 2 * COLS, bytes_accessed=10 << 20, transcendentals=0
        ),
        name=f"project_{head}",
    )(offs, mixed, *pieces)


def finish_kernel(meta_ref, *refs):
    x_refs = refs[:4]
    near_ref, near_in_ref = refs[4:6]
    far_refs = refs[6:8]
    far_in_refs = refs[8:10]
    weight_ref, hidden_ref, score_ref, acc_ref = refs[10:]
    weight = weight_ref[...]
    place = lax.broadcasted_iota(jnp.int32, (RECLEN, 1), 0)
    lane = lax.broadcasted_iota(jnp.int32, (1, 128), 1)
    token = lax.broadcasted_iota(jnp.int32, (TOK, RECLEN), 0)
    slot = lax.broadcasted_iota(jnp.int32, (TOK, RECLEN), 1)
    scores = jnp.zeros((1, 128), jnp.float32)
    for i in range(4):
        row, start, length = meta_ref[i], meta_ref[4 + i], meta_ref[8 + i]
        mine = pl.ds(i * RECLEN, RECLEN)
        theirs = pl.ds((i ^ 1) * RECLEN, RECLEN)
        far = pl.ds((i % 2) * RECLEN, RECLEN)
        far_in = pl.ds((1 - i % 2) * RECLEN, RECLEN)
        total = (
            x_refs[i][...].astype(jnp.float32)
            + near_ref[mine, :].astype(jnp.float32)
            + near_in_ref[theirs, :].astype(jnp.float32)
            + far_refs[i // 2][far, :].astype(jnp.float32)
            + far_in_refs[i // 2][far_in, :].astype(jnp.float32)
        )
        token_score = jnp.sum(total * weight, axis=1, keepdims=True)
        score = jnp.sum(jnp.where(place < length, token_score, 0.0), axis=0, keepdims=True)
        scores = scores + jnp.where(lane == row, score, 0.0)
        pick = ((token - slot == start) & (slot < length)).astype(jnp.bfloat16)
        moved = jnp.dot(pick, total.astype(jnp.bfloat16), preferred_element_type=jnp.float32)
        if i == 0:
            acc_ref[...] = moved
        else:
            acc_ref[...] += moved
    hidden_ref[...] = acc_ref[...].astype(jnp.bfloat16)
    score_ref[...] = scores


def finish(meta, records, near, near_in, fars, fars_in, weight):
    def whole(a):
        return pl.BlockSpec(a.shape, lambda i, m: (0,) * a.ndim)

    slices = pl.BlockSpec((RECLEN, COLS), lambda i, m: (0, m[12]))
    return pl.pallas_call(
        finish_kernel,
        out_shape=[
            jax.ShapeDtypeStruct((TOK, COLS), jnp.bfloat16),
            jax.ShapeDtypeStruct((1, 128), jnp.float32),
        ],
        grid_spec=pltpu.PrefetchScalarGridSpec(
            num_scalar_prefetch=1,
            grid=(1,),
            in_specs=[slices] * 4
            + [whole(near), whole(near_in)]
            + [whole(f) for f in (*fars, *fars_in)]
            + [pl.BlockSpec((1, COLS), lambda i, m: (0, m[12]))],
            out_specs=[
                pl.BlockSpec((TOK, COLS), lambda i, m: (0, 0)),
                pl.BlockSpec((1, 128), lambda i, m: (0, 0)),
            ],
            scratch_shapes=[pltpu.VMEM((TOK, COLS), jnp.float32)],
        ),
        compiler_params=pltpu.CompilerParams(vmem_limit_bytes=VMEM_LIMIT),
        cost_estimate=pl.CostEstimate(
            flops=2 * TOK * 4 * RECLEN * COLS, bytes_accessed=16 << 20, transcendentals=0
        ),
        name="finish",
    )(meta, *records, near, near_in, *fars, *fars_in, weight)


def on_device(records, lengths, assignment, segment_ids, norm_gain, w_qkv, w_out, score_weights):
    xh, co, xl, z, y = (lax.axis_index(a) for a in ("xh", "co", "xl", "z", "y"))
    row_index = xh * 2 + co
    reader_index = xl * 16 + z * 4 + y
    swap_xl, swap_xh, swap_co = ring("xl", 2, 1), ring("xh", 2, 1), ring("co", 2, 1)
    rec_ids = jnp.arange(32, dtype=jnp.int32)

    own_assign = lax.dynamic_index_in_dim(assignment, row_index, 0, keepdims=False)
    outgoing = jnp.sum(
        jnp.where(own_assign[None, :] == rec_ids[:, None], rec_ids[None, :], 0), axis=1
    )
    send_block = order_records(outgoing, records.reshape(32, 8, WIDTH))
    arrived = lax.all_to_all(
        send_block, ("xl", "z", "y"), split_axis=0, concat_axis=0, tiled=True
    )
    own_record = arrived.reshape(RECLEN, WIDTH)
    peer_record = swap_co(own_record)
    far_record = swap_xh(own_record)
    far_peer_record = swap_co(far_record)
    slots = [own_record, peer_record, far_record, far_peer_record]

    chosen = assignment == reader_index
    row_order = jnp.stack(
        [row_index, row_index + 1 - 2 * co, row_index + 2 - 4 * xh, 3 - row_index]
    )
    pick_row = row_order[:, None] == jnp.arange(4, dtype=jnp.int32)[None, :]
    lens = jnp.sum(jnp.where(chosen, lengths, 0), axis=1)
    segs = jnp.sum(jnp.where(chosen[:, :, None], segment_ids, 0), axis=1)
    local_lens = jnp.sum(jnp.where(pick_row, lens[None, :], 0), axis=1)
    before = jnp.arange(4, dtype=jnp.int32)[None, :] < row_order[:, None]
    local_starts = jnp.sum(jnp.where(before, lens[None, :], 0), axis=1)
    local_segs = jnp.sum(jnp.where(pick_row[:, :, None], segs[None], 0), axis=1)
    segq = local_segs[:, :, None]
    segk = local_segs[:, None, :]
    meta = jnp.concatenate([row_order, local_starts, local_lens, row_index[None]])

    inv_freq = ROPE_BASE ** (-(jnp.arange(HS // 2, dtype=jnp.float32) * 2.0 / HS))
    angle = jnp.arange(RECLEN, dtype=jnp.float32)[:, None] * inv_freq[None, :]
    cosine = jnp.cos(angle)
    sine = jnp.sin(angle)
    cosine = jnp.concatenate([cosine, cosine], axis=1)
    sine = jnp.concatenate([-sine, sine], axis=1)

    w_own = w_qkv.reshape(BLK, QKV)
    w_peer = swap_xl(w_own)
    qkv_pieces = plane_gather_second(plane_gather_first(w_own)) + plane_gather_second(
        plane_gather_first(w_peer)
    )

    o_own = w_out.reshape(BLK, HEADS)
    o_peer = swap_xl(o_own)
    here = xl == xh
    o_near = jnp.where(here, o_own, o_peer)
    o_far = swap_xh(jnp.where(here, o_peer, o_own))
    out_pieces = plane_gather_second(
        plane_gather_first(jnp.concatenate([o_near, o_far], axis=0))
    )

    steps_a = jnp.arange(4, dtype=jnp.int32)[:, None]
    steps_b = jnp.arange(4, dtype=jnp.int32)[None, :]
    src_z = jnp.where(co == 0, z - steps_b, z - steps_a) & 3
    src_y = jnp.where(co == 0, y - steps_a, y - steps_b) & 3
    plane = (src_z * 4 + src_y).reshape(16)
    qkv_offs = BLK * jnp.concatenate([xl * 16 + plane, (1 - xl) * 16 + plane])
    kept = ((src_z // 2) == co).astype(jnp.int32)
    out_offs = (kept * COLS + (src_z & 1) * (4 * BLK) + src_y * BLK).reshape(16)

    gain = norm_gain[None, :]
    mixed_a = attend(
        qkv_offs, slots[0], slots[1], gain, cosine, sine, segq[:2], segk[:2], qkv_pieces
    )
    mixed_b = attend(
        qkv_offs, slots[2], slots[3], gain, cosine, sine, segq[2:], segk[2:], qkv_pieces
    )
    far_b = swap_xh(mixed_a)
    far_a = swap_xh(mixed_b)
    near_away, near_kept = project(
        out_offs, jnp.concatenate([mixed_a, mixed_b], axis=0), out_pieces, 0
    )
    near_in = swap_co(near_away)
    away_b, kept_b = project(out_offs, far_b, out_pieces, 1)
    in_b = swap_co(away_b)
    away_a, kept_a = project(out_offs, far_a, out_pieces, 1)
    in_a = swap_co(away_a)
    hidden_out, scores = finish(
        meta, slots, near_kept, near_in, (kept_a, kept_b), (in_a, in_b), score_weights[None, :]
    )
    scores = lax.psum(scores[0, :4], ("xh", "co"))
    record_scores = (scores / lens.astype(jnp.float32))[None, :]
    return (hidden_out, record_scores)


def solution(mesh):
    fine = Mesh(mesh.devices.reshape(2, 2, 2, 4, 4), ("xh", "co", "xl", "z", "y"))
    row, reader = ("xh", "co"), ("xl", "z", "y")
    in_specs = (
        P(row, None, reader, None),
        P(),
        P(),
        P(),
        P(),
        P(reader, row, None),
        P(reader, row, None),
        P(),
    )
    out_specs = (P(reader, row), P(reader, None))
    return jax.shard_map(
        on_device, mesh=fine, in_specs=in_specs, out_specs=out_specs, check_vma=False
    )
```

```python
import math

import jax
import jax.numpy as jnp
from jax import lax
from jax.experimental import pallas as pl
from jax.experimental.pallas import tpu as pltpu
from jax.sharding import Mesh, PartitionSpec as P

HS = 128
GROUP = 8
RECLEN = 256
WIDTH = 4096
TOK = 896
QKV = (GROUP + 2) * HS
HEADS = GROUP * HS
COLS = WIDTH // 4
ROPE_BASE = 500000.0
BLK = 128
QBLK = 256
ATTEND_VMEM = 16 << 20
SMALL_VMEM = 12 << 20
PROJECT_VMEM = 16 << 20
FINISH_VMEM = 28 << 20

CORE_ZY = ("co", "z", "y")


def ring(axis, size, step):
    return lambda v: lax.ppermute(v, axis, [(i, (i + step) % size) for i in range(size)])


def plane_perm(step, first):
    pairs = []
    for co in range(2):
        for z in range(4):
            for y in range(4):
                along_y = (co == 0) == first
                z2, y2 = (z, (y + step) % 4) if along_y else ((z + step) % 4, y)
                pairs.append((co * 16 + z * 4 + y, co * 16 + z2 * 4 + y2))
    return lambda v: lax.ppermute(v, CORE_ZY, pairs)


def stack_kernel(plan, *refs):
    out_ref = refs[-1]
    to = 0
    for which, row, rows in plan:
        out_ref[to : to + rows] = refs[which][row : row + rows]
        to += rows


def stack(arrays, plan, after=None):
    rows = sum(p[2] for p in plan)
    held = [] if after is None else after if isinstance(after, list) else [after]
    return pl.pallas_call(
        lambda *refs: stack_kernel(plan, *refs),
        out_shape=jax.ShapeDtypeStruct((rows, arrays[0].shape[1]), arrays[0].dtype),
        in_specs=[pl.BlockSpec(memory_space=pltpu.VMEM)] * len(arrays)
        + [pl.BlockSpec(memory_space=pl.ANY)] * len(held),
        out_specs=pl.BlockSpec(memory_space=pltpu.VMEM),
        compiler_params=pltpu.CompilerParams(vmem_limit_bytes=SMALL_VMEM),
        cost_estimate=pl.CostEstimate(flops=0, bytes_accessed=1 << 20, transcendentals=0),
        name="stack",
    )(*arrays, *held)


def plane_gather_first(block, groups, after=None):
    one = plane_perm(1, True)(block)
    three = plane_perm(-1, True)(block)
    two = plane_perm(2, True)(block)
    plan = [(i, g * BLK, BLK) for g in range(groups) for i in range(4)]
    return stack([block, one, two, three], plan, after)


def plane_gather_second(line):
    half = line.shape[0] // 2
    one = plane_perm(1, False)(line)
    three = plane_perm(-1, False)(line)
    two_a = plane_perm(1, False)(one[:half])
    two_b = plane_perm(-1, False)(three[half:])
    return [line, one, three, two_a, two_b]


def order_kernel(outgoing_ref, records_ref, *rest):
    out_ref, sems = rest[-2:]
    copies = [
        pltpu.make_async_copy(records_ref.at[outgoing_ref[j]], out_ref.at[j], sems.at[j])
        for j in range(32)
    ]
    for copy in copies:
        copy.start()
    for copy in copies:
        copy.wait()


def order_records(outgoing, records, after):
    return pl.pallas_call(
        order_kernel,
        out_shape=jax.ShapeDtypeStruct(records.shape, records.dtype),
        in_specs=[pl.BlockSpec(memory_space=pltpu.SMEM)]
        + [pl.BlockSpec(memory_space=pl.ANY)] * (1 + len(after)),
        out_specs=pl.BlockSpec(memory_space=pltpu.VMEM),
        scratch_shapes=[pltpu.SemaphoreType.DMA((32,))],
        cost_estimate=pl.CostEstimate(flops=0, bytes_accessed=4 << 20, transcendentals=0),
        name="order_records",
    )(outgoing, records, *after)


def normalize_kernel(offs_ref, xa_ref, xb_ref, gain_ref, normed_ref):
    for part, x_ref in enumerate((xa_ref, xb_ref)):

        @pl.loop(0, RECLEN // 32)
        def _(i, part=part, x_ref=x_ref):
            rows = pl.ds(pl.multiple_of(i * 32, 32), 32)
            into = pl.ds(pl.multiple_of(part * RECLEN + i * 32, 32), 32)
            x = x_ref[rows, :].astype(jnp.float32)
            scale = lax.rsqrt(jnp.mean(x * x, axis=1, keepdims=True) + 1e-05)
            for n in range(32):
                cols = pl.ds(pl.multiple_of(offs_ref[n], BLK), BLK)
                normed_ref[into, n * BLK : (n + 1) * BLK] = (
                    x_ref[rows, cols].astype(jnp.float32) * scale * gain_ref[:, cols]
                ).astype(jnp.bfloat16)


def normalize(offs, xa, xb, gain):
    vmem = pl.BlockSpec(memory_space=pltpu.VMEM)
    return pl.pallas_call(
        normalize_kernel,
        out_shape=jax.ShapeDtypeStruct((2 * RECLEN, WIDTH), jnp.bfloat16),
        in_specs=[pl.BlockSpec(memory_space=pltpu.SMEM)] + [vmem] * 3,
        out_specs=vmem,
        compiler_params=pltpu.CompilerParams(vmem_limit_bytes=SMALL_VMEM),
        cost_estimate=pl.CostEstimate(
            flops=2 * 512 * WIDTH, bytes_accessed=12 << 20, transcendentals=0
        ),
        name="normalize",
    )(offs, xa, xb, gain)


def attend_kernel(normed_ref, cos_ref, sin_ref, segq_ref, segk_ref, *rest):
    pieces = rest[:10]
    out_ref, proj_ref = rest[-2:]

    @pl.loop(0, QKV // 256)
    def _(n):
        cols = pl.ds(pl.multiple_of(n * 256, 256), 256)
        total, start = 0.0, 0
        for piece in pieces:
            stop = start + piece.shape[0]
            total += jnp.dot(
                normed_ref[:, start:stop], piece[:, cols], preferred_element_type=jnp.float32
            )
            start = stop
        proj_ref[:, cols] = total

    cosine = cos_ref[...]
    sine = sin_ref[...]
    place_k = lax.broadcasted_iota(jnp.int32, (RECLEN, RECLEN), 0)
    place_q = lax.broadcasted_iota(jnp.int32, (RECLEN, RECLEN), 1)
    scaling = math.log2(math.e) / math.sqrt(HS)
    ones = jnp.ones((16, RECLEN), jnp.bfloat16)
    for part in range(2):
        rows = slice(part * RECLEN, (part + 1) * RECLEN)
        allowed = (segq_ref[part] == segk_ref[part]) & (place_k <= place_q)
        key = proj_ref[rows, GROUP * HS : (GROUP + 1) * HS]
        key = key * cosine + pltpu.roll(key, HS // 2, 1) * sine
        key = jnp.concatenate([key, pltpu.roll(key, HS // 2, 1)], axis=1).astype(jnp.bfloat16)
        value = proj_ref[rows, (GROUP + 1) * HS : (GROUP + 2) * HS].T.astype(jnp.bfloat16)
        value = jnp.concatenate([value, ones], axis=0)
        for g in range(GROUP):
            cols = slice(g * HS, (g + 1) * HS)
            query = proj_ref[rows, cols]
            query = jnp.concatenate([query * cosine, -(query * sine)], axis=1).astype(jnp.bfloat16)
            for low in range(0, RECLEN, QBLK):
                high = low + QBLK
                logits = lax.dot_general(
                    key[:high],
                    query[low:high],
                    (((1,), (1,)), ((), ())),
                    preferred_element_type=jnp.float32,
                )
                held = jnp.where(allowed[:high, low:high], logits, -1e30)
                top = jnp.max(held, axis=0, keepdims=True)
                weights = jnp.exp2((held - top) * scaling).astype(jnp.bfloat16)
                mixed = jnp.dot(value[:, :high], weights, preferred_element_type=jnp.float32)
                mixed = mixed[:HS] / mixed[HS : HS + 1]
                out_ref[rows.start + low : rows.start + high, cols] = mixed.T.astype(jnp.bfloat16)


def attend(normed, cosine, sine, segq, segk, pieces, after=()):
    vmem = pl.BlockSpec(memory_space=pltpu.VMEM)
    return pl.pallas_call(
        attend_kernel,
        out_shape=jax.ShapeDtypeStruct((2 * RECLEN, HEADS), jnp.bfloat16),
        in_specs=[vmem] * 15 + [pl.BlockSpec(memory_space=pl.ANY)] * len(after),
        out_specs=vmem,
        scratch_shapes=[pltpu.VMEM((2 * RECLEN, QKV), jnp.float32)],
        compiler_params=pltpu.CompilerParams(vmem_limit_bytes=ATTEND_VMEM),
        cost_estimate=pl.CostEstimate(
            flops=2 * 512 * WIDTH * QKV, bytes_accessed=16 << 20, transcendentals=1 << 20
        ),
        name="attend",
    )(normed, cosine, sine, segq, segk, *pieces, *after)


def arrange_kernel(head, offs_ref, line_ref, one_ref, three_ref, two_ref, out_ref, raw_ref, sems):
    copies = []
    for b, piece in enumerate((line_ref, one_ref, two_ref, three_ref)):
        for a in range(4):
            n = a * 4 + b
            row = a * BLK if b == 2 else (head * 4 + a) * BLK
            to = pl.multiple_of(offs_ref[n], BLK)
            copies.append(
                pltpu.make_async_copy(
                    piece.at[pl.ds(row, BLK)], raw_ref.at[pl.ds(to, BLK)], sems.at[n]
                )
            )
    for copy in copies:
        copy.start()
    for copy in copies:
        copy.wait()

    @pl.loop(0, 2 * COLS // 256)
    def _(n):
        rows = pl.ds(pl.multiple_of(n * 256, 256), 256)
        out_ref[:, rows] = raw_ref[rows, :].T


def arrange(offs, pieces, head):
    line, one, three, two_a, two_b = pieces
    return pl.pallas_call(
        lambda *refs: arrange_kernel(head, *refs),
        out_shape=jax.ShapeDtypeStruct((HEADS, 2 * COLS), jnp.bfloat16),
        in_specs=[pl.BlockSpec(memory_space=pltpu.SMEM)]
        + [pl.BlockSpec(memory_space=pl.ANY)] * 4,
        out_specs=pl.BlockSpec(memory_space=pltpu.VMEM),
        scratch_shapes=[
            pltpu.VMEM((2 * COLS, HEADS), jnp.bfloat16),
            pltpu.SemaphoreType.DMA((16,)),
        ],
        compiler_params=pltpu.CompilerParams(vmem_limit_bytes=SMALL_VMEM),
        cost_estimate=pl.CostEstimate(flops=0, bytes_accessed=8 << 20, transcendentals=0),
        name=f"arrange_{head}",
    )(offs, line, one, three, two_b if head else two_a)


def project_kernel(first, mixed_ref, w_ref, *rest):
    out_refs = rest[-3:-1]
    for part, out_ref in enumerate(out_refs):

        @pl.loop(0, COLS // 256)
        def _(n, part=part, out_ref=out_ref):
            from_cols = pl.ds(pl.multiple_of(part * COLS + n * 256, 256), 256)
            cols = pl.ds(pl.multiple_of(n * 256, 256), 256)
            out_ref[:, cols] = jnp.dot(
                mixed_ref[...], w_ref[:, from_cols], preferred_element_type=jnp.float32
            ).astype(jnp.bfloat16)

    meta_ref, weight_ref, score_ref = rest[0], rest[1], rest[-1]
    token = jnp.zeros((2 * RECLEN, 1), jnp.float32)
    for part, out_ref in enumerate(out_refs):
        terms = out_ref[...].astype(jnp.float32) * weight_ref[part : part + 1, :]
        token += jnp.sum(terms, axis=1, keepdims=True)
    score_ref[...] = row_scores(token, meta_ref, first, 2)


def project(mixed, w, meta, weight, first):
    vmem = pl.BlockSpec(memory_space=pltpu.VMEM)
    tokens = mixed.shape[0]
    return pl.pallas_call(
        lambda *refs: project_kernel(first, *refs),
        out_shape=[jax.ShapeDtypeStruct((tokens, COLS), jnp.bfloat16)] * 2
        + [jax.ShapeDtypeStruct((1, 128), jnp.float32)],
        in_specs=[vmem] * 2 + [pl.BlockSpec(memory_space=pltpu.SMEM), vmem],
        out_specs=[vmem] * 3,
        compiler_params=pltpu.CompilerParams(vmem_limit_bytes=PROJECT_VMEM),
        cost_estimate=pl.CostEstimate(
            flops=2 * tokens * HEADS * 2 * COLS, bytes_accessed=2 << 20, transcendentals=0
        ),
        name="project",
    )(mixed, w, meta, weight)


def row_scores(token, place_ref, first, count):
    slot = lax.broadcasted_iota(jnp.int32, (RECLEN, 1), 0)
    lane = lax.broadcasted_iota(jnp.int32, (1, 128), 1)
    scores = jnp.zeros((1, 128), jnp.float32)
    for i in range(count):
        row, length = place_ref[first + i], place_ref[8 + first + i]
        used = jnp.where(slot < length, token[i * RECLEN : (i + 1) * RECLEN], 0.0)
        scores += jnp.where(lane == row, jnp.sum(used, axis=0, keepdims=True), 0.0)
    return scores


def packed_rows(meta_ref, i, total):
    start, length = meta_ref[4 + i], meta_ref[8 + i]
    token = lax.broadcasted_iota(jnp.int32, (TOK, RECLEN), 0)
    slot = lax.broadcasted_iota(jnp.int32, (TOK, RECLEN), 1)
    pick = ((token - slot == start) & (slot < length)).astype(jnp.bfloat16)
    return jnp.dot(pick, total.astype(jnp.bfloat16), preferred_element_type=jnp.float32)


def finish_kernel(meta_ref, *refs):
    x_refs, kept_refs, in_refs = refs[:4], refs[4:8], refs[8:12]
    hidden_ref, acc_ref = refs[12:]
    for i in range(4):
        mine = slice(i % 2 * RECLEN, (i % 2 + 1) * RECLEN)
        theirs = slice((1 - i % 2) * RECLEN, (2 - i % 2) * RECLEN)
        total = x_refs[i][...].astype(jnp.float32)
        for head in range(2):
            n = i // 2 * 2 + head
            total += kept_refs[n][mine, :].astype(jnp.float32)
            total += in_refs[n][theirs, :].astype(jnp.float32)
        moved = packed_rows(meta_ref, i, total)
        if i == 0:
            acc_ref[...] = moved
        elif i < 3:
            acc_ref[...] += moved
        else:
            hidden_ref[...] = (acc_ref[...] + moved).astype(jnp.bfloat16)


def finish(meta, records, kept, swapped):
    def whole(shape):
        return pl.BlockSpec(shape, lambda i, m: (0,) * len(shape))

    slices = pl.BlockSpec((RECLEN, COLS), lambda i, m: (0, m[12]))
    return pl.pallas_call(
        finish_kernel,
        out_shape=jax.ShapeDtypeStruct((TOK, COLS), jnp.bfloat16),
        grid_spec=pltpu.PrefetchScalarGridSpec(
            num_scalar_prefetch=1,
            grid=(1,),
            in_specs=[slices] * 4 + [whole(v.shape) for v in (*kept, *swapped)],
            out_specs=whole((TOK, COLS)),
            scratch_shapes=[pltpu.VMEM((TOK, COLS), jnp.float32)],
        ),
        compiler_params=pltpu.CompilerParams(vmem_limit_bytes=FINISH_VMEM),
        cost_estimate=pl.CostEstimate(
            flops=2 * TOK * 4 * RECLEN * COLS, bytes_accessed=16 << 20, transcendentals=0
        ),
        name="finish",
    )(meta, *records, *kept, *swapped)


def record_score_kernel(meta_ref, record_ref, weight_ref, score_ref):
    token = jnp.sum(
        record_ref[...].astype(jnp.float32) * weight_ref[...], axis=1, keepdims=True
    )
    score_ref[...] = row_scores(token, meta_ref, 0, 1)


def record_score(meta, record, weight):
    vmem = pl.BlockSpec(memory_space=pltpu.VMEM)
    return pl.pallas_call(
        record_score_kernel,
        out_shape=jax.ShapeDtypeStruct((1, 128), jnp.float32),
        in_specs=[pl.BlockSpec(memory_space=pltpu.SMEM), vmem, vmem],
        out_specs=vmem,
        compiler_params=pltpu.CompilerParams(vmem_limit_bytes=SMALL_VMEM),
        cost_estimate=pl.CostEstimate(flops=2 << 20, bytes_accessed=2 << 20, transcendentals=0),
        name="record_score",
    )(meta, record, weight)


def on_device(records, lengths, assignment, segment_ids, norm_gain, w_qkv, w_out, score_weights):
    xh, co, xl, z, y = (lax.axis_index(a) for a in ("xh", "co", "xl", "z", "y"))
    row_index = xh * 2 + co
    reader_index = xl * 16 + z * 4 + y
    swap_xl, swap_xh, swap_co = ring("xl", 2, 1), ring("xh", 2, 1), ring("co", 2, 1)
    rec_ids = jnp.arange(32, dtype=jnp.int32)

    o_own = w_out.reshape(BLK, HEADS)
    here = xl == xh
    o_peer = swap_xl(o_own)
    o_across = lax.ppermute(o_own, ("xh", "xl"), [(0, 2), (2, 0), (1, 3), (3, 1)])
    o_corner = lax.ppermute(o_own, ("xh", "xl"), [(0, 3), (3, 0), (1, 2), (2, 1)])
    o_both = jnp.concatenate(
        [jnp.where(here, o_own, o_peer), jnp.where(here, o_across, o_corner)], axis=0
    )

    w_own = w_qkv.reshape(BLK, QKV)
    w_peer = swap_xl(w_own)
    own_line = plane_gather_first(w_own, 1)

    own_assign = lax.dynamic_index_in_dim(assignment, row_index, 0, keepdims=False)
    outgoing = jnp.sum(
        jnp.where(own_assign[None, :] == rec_ids[:, None], rec_ids[None, :], 0), axis=1
    )
    send_block = order_records(outgoing, records.reshape(32, 8, WIDTH), [o_both, own_line, w_peer])
    arrived = lax.all_to_all(
        send_block, ("xl", "z", "y"), split_axis=0, concat_axis=0, tiled=True
    )
    own_record = arrived.reshape(RECLEN, WIDTH)
    peer_record = swap_co(own_record)

    own_pieces = plane_gather_second(stack([own_line], [(0, 0, 4 * BLK)], own_record))
    peer_pieces = plane_gather_second(
        plane_gather_first(stack([w_peer], [(0, 0, BLK)], own_record), 1)
    )
    qkv_pieces = own_pieces + peer_pieces
    o_both = stack([o_both], [(0, 0, 2 * BLK)], peer_pieces[3:] + own_pieces[3:])
    out_pieces = plane_gather_second(plane_gather_first(o_both, 2))

    far_record = stack([swap_xh(own_record)], [(0, 0, RECLEN)], peer_pieces[1:3])
    far_peer_record = swap_co(far_record)
    slots = [own_record, peer_record, far_record, far_peer_record]

    chosen = assignment == reader_index
    row_order = jnp.stack(
        [row_index, row_index + 1 - 2 * co, row_index + 2 - 4 * xh, 3 - row_index]
    )
    pick_row = row_order[:, None] == jnp.arange(4, dtype=jnp.int32)[None, :]
    lens = jnp.sum(jnp.where(chosen, lengths, 0), axis=1)
    segs = jnp.sum(jnp.where(chosen[:, :, None], segment_ids, 0), axis=1)
    local_lens = jnp.sum(jnp.where(pick_row, lens[None, :], 0), axis=1)
    before = jnp.arange(4, dtype=jnp.int32)[None, :] < row_order[:, None]
    local_starts = jnp.sum(jnp.where(before, lens[None, :], 0), axis=1)
    local_segs = jnp.sum(jnp.where(pick_row[:, :, None], segs[None], 0), axis=1)
    segq = local_segs[:, :, None]
    segk = local_segs[:, None, :]
    meta = jnp.concatenate([row_order, local_starts, local_lens, row_index[None]])

    inv_freq = ROPE_BASE ** (-(jnp.arange(HS // 2, dtype=jnp.float32) * 2.0 / HS))
    angle = jnp.arange(RECLEN, dtype=jnp.float32)[:, None] * inv_freq[None, :]
    cosine = jnp.cos(angle)
    sine = jnp.sin(angle)
    cosine = jnp.concatenate([cosine, cosine], axis=1)
    sine = jnp.concatenate([-sine, sine], axis=1)


    steps_a = jnp.arange(4, dtype=jnp.int32)[:, None]
    steps_b = jnp.arange(4, dtype=jnp.int32)[None, :]
    src_z = jnp.where(co == 0, z - steps_b, z - steps_a) & 3
    src_y = jnp.where(co == 0, y - steps_a, y - steps_b) & 3
    plane = BLK * (src_z * 4 + src_y)
    plane = jnp.stack([plane[:, b] for b in (0, 1, 3, 2)]).reshape(16)
    qkv_offs = jnp.concatenate([xl * 2048 + plane, (1 - xl) * 2048 + plane])
    kept = ((src_z // 2) == co).astype(jnp.int32)
    out_offs = (kept * COLS + (src_z & 1) * (4 * BLK) + src_y * BLK).reshape(16)

    gain = norm_gain[None, :]
    normed_a = normalize(qkv_offs, slots[0], slots[1], gain)
    normed_b = normalize(qkv_offs, slots[2], slots[3], gain)
    mixed_a = attend(normed_a, cosine, sine, segq[:2], segk[:2], qkv_pieces, [normed_b])
    mixed_b = attend(normed_b, cosine, sine, segq[2:], segk[2:], qkv_pieces)
    far_b = swap_xh(mixed_a)
    far_a = swap_xh(mixed_b)
    weights = score_weights.reshape(4, COLS)
    weight = jnp.stack(
        [
            lax.dynamic_index_in_dim(weights, row_index + 1 - 2 * co, 0, keepdims=False),
            lax.dynamic_index_in_dim(weights, row_index, 0, keepdims=False),
        ]
    )
    w_near, w_far = arrange(out_offs, out_pieces, 0), arrange(out_offs, out_pieces, 1)

    terms = [
        project(mixed_a, w_near, meta, weight, 0),
        project(far_a, w_far, meta, weight, 0),
        project(mixed_b, w_near, meta, weight, 2),
        project(far_b, w_far, meta, weight, 2),
    ]
    hidden_out = finish(meta, slots, [t[1] for t in terms], [swap_co(t[0]) for t in terms])
    partial = record_score(meta, own_record, score_weights[None, :])
    partial += (terms[0][2] + terms[2][2]) + (terms[3][2] + terms[1][2])
    scores = lax.psum(partial[0, :4], ("xh", "co"))
    record_scores = (scores / lens.astype(jnp.float32))[None, :]
    return (hidden_out, record_scores)


def solution(mesh):
    fine = Mesh(mesh.devices.reshape(2, 2, 2, 4, 4), ("xh", "co", "xl", "z", "y"))
    row, reader = ("xh", "co"), ("xl", "z", "y")
    in_specs = (
        P(row, None, reader, None),
        P(),
        P(),
        P(),
        P(),
        P(reader, row, None),
        P(reader, row, None),
        P(),
    )
    out_specs = (P(reader, row), P(reader, None))
    return jax.shard_map(
        on_device, mesh=fine, in_specs=in_specs, out_specs=out_specs, check_vma=False
    )
```

```python
import math

import jax
import jax.numpy as jnp
from jax import lax
from jax.experimental import pallas as pl
from jax.experimental.pallas import tpu as pltpu
from jax.sharding import Mesh, PartitionSpec as P

HS = 128
GROUP = 8
RECLEN = 256
WIDTH = 4096
TOK = 896
QKV = (GROUP + 2) * HS
HEADS = GROUP * HS
COLS = WIDTH // 4
ROPE_BASE = 500000.0
BLK = 128
QBLK = 256
ATTEND_VMEM = 16 << 20
SMALL_VMEM = 12 << 20
PROJECT_VMEM = 16 << 20
FINISH_VMEM = 28 << 20

CORE_ZY = ("co", "z", "y")


def ring(axis, size, step):
    return lambda v: lax.ppermute(v, axis, [(i, (i + step) % size) for i in range(size)])


def plane_perm(step, first):
    pairs = []
    for co in range(2):
        for z in range(4):
            for y in range(4):
                along_y = (co == 0) == first
                z2, y2 = (z, (y + step) % 4) if along_y else ((z + step) % 4, y)
                pairs.append((co * 16 + z * 4 + y, co * 16 + z2 * 4 + y2))
    return lambda v: lax.ppermute(v, CORE_ZY, pairs)


def stack_kernel(plan, *refs):
    out_ref = refs[-1]
    to = 0
    for which, row, rows in plan:
        out_ref[to : to + rows] = refs[which][row : row + rows]
        to += rows


def stack(arrays, plan, after=None):
    rows = sum(p[2] for p in plan)
    held = [] if after is None else after if isinstance(after, list) else [after]
    return pl.pallas_call(
        lambda *refs: stack_kernel(plan, *refs),
        out_shape=jax.ShapeDtypeStruct((rows, arrays[0].shape[1]), arrays[0].dtype),
        in_specs=[pl.BlockSpec(memory_space=pltpu.VMEM)] * len(arrays)
        + [pl.BlockSpec(memory_space=pl.ANY)] * len(held),
        out_specs=pl.BlockSpec(memory_space=pltpu.VMEM),
        compiler_params=pltpu.CompilerParams(vmem_limit_bytes=SMALL_VMEM),
        cost_estimate=pl.CostEstimate(flops=0, bytes_accessed=1 << 20, transcendentals=0),
        name="stack",
    )(*arrays, *held)


def plane_gather_first(block, groups, after=None):
    one = plane_perm(1, True)(block)
    three = plane_perm(-1, True)(block)
    two = plane_perm(2, True)(block)
    plan = [(i, g * BLK, BLK) for g in range(groups) for i in range(4)]
    return stack([block, one, two, three], plan, after)


def plane_gather_second(line):
    half = line.shape[0] // 2
    one = plane_perm(1, False)(line)
    three = plane_perm(-1, False)(line)
    two_a = plane_perm(1, False)(one[:half])
    two_b = plane_perm(-1, False)(three[half:])
    return [line, one, three, two_a, two_b]


def order_kernel(outgoing_ref, records_ref, *rest):
    out_ref, sems = rest[-2:]
    copies = [
        pltpu.make_async_copy(records_ref.at[outgoing_ref[j]], out_ref.at[j], sems.at[j])
        for j in range(32)
    ]
    for copy in copies:
        copy.start()
    for copy in copies:
        copy.wait()


def order_records(outgoing, records, after):
    return pl.pallas_call(
        order_kernel,
        out_shape=jax.ShapeDtypeStruct(records.shape, records.dtype),
        in_specs=[pl.BlockSpec(memory_space=pltpu.SMEM)]
        + [pl.BlockSpec(memory_space=pl.ANY)] * (1 + len(after)),
        out_specs=pl.BlockSpec(memory_space=pltpu.VMEM),
        scratch_shapes=[pltpu.SemaphoreType.DMA((32,))],
        cost_estimate=pl.CostEstimate(flops=0, bytes_accessed=4 << 20, transcendentals=0),
        name="order_records",
    )(outgoing, records, *after)


def normalize_kernel(offs_ref, xa_ref, xb_ref, gain_ref, normed_ref):
    for part, x_ref in enumerate((xa_ref, xb_ref)):

        @pl.loop(0, RECLEN // 32)
        def _(i, part=part, x_ref=x_ref):
            rows = pl.ds(pl.multiple_of(i * 32, 32), 32)
            into = pl.ds(pl.multiple_of(part * RECLEN + i * 32, 32), 32)
            x = x_ref[rows, :].astype(jnp.float32)
            scale = lax.rsqrt(jnp.mean(x * x, axis=1, keepdims=True) + 1e-05)
            for n in range(32):
                cols = pl.ds(pl.multiple_of(offs_ref[n], BLK), BLK)
                normed_ref[into, n * BLK : (n + 1) * BLK] = (
                    x_ref[rows, cols].astype(jnp.float32) * scale * gain_ref[:, cols]
                ).astype(jnp.bfloat16)


def normalize(offs, xa, xb, gain):
    vmem = pl.BlockSpec(memory_space=pltpu.VMEM)
    return pl.pallas_call(
        normalize_kernel,
        out_shape=jax.ShapeDtypeStruct((2 * RECLEN, WIDTH), jnp.bfloat16),
        in_specs=[pl.BlockSpec(memory_space=pltpu.SMEM)] + [vmem] * 3,
        out_specs=vmem,
        compiler_params=pltpu.CompilerParams(vmem_limit_bytes=SMALL_VMEM),
        cost_estimate=pl.CostEstimate(
            flops=2 * 512 * WIDTH, bytes_accessed=12 << 20, transcendentals=0
        ),
        name="normalize",
    )(offs, xa, xb, gain)


def attend_kernel(normed_ref, cos_ref, sin_ref, segq_ref, segk_ref, *rest):
    pieces = rest[:10]
    out_ref, proj_ref = rest[-2:]

    @pl.loop(0, QKV // 256)
    def _(n):
        cols = pl.ds(pl.multiple_of(n * 256, 256), 256)
        total, start = 0.0, 0
        for piece in pieces:
            stop = start + piece.shape[0]
            total += jnp.dot(
                normed_ref[:, start:stop], piece[:, cols], preferred_element_type=jnp.float32
            )
            start = stop
        proj_ref[:, cols] = total

    cosine = cos_ref[...]
    sine = sin_ref[...]
    place_k = lax.broadcasted_iota(jnp.int32, (RECLEN, RECLEN), 0)
    place_q = lax.broadcasted_iota(jnp.int32, (RECLEN, RECLEN), 1)
    scaling = math.log2(math.e) / math.sqrt(HS)
    ones = jnp.ones((16, RECLEN), jnp.bfloat16)
    for part in range(2):
        rows = slice(part * RECLEN, (part + 1) * RECLEN)
        allowed = (segq_ref[part] == segk_ref[part]) & (place_k <= place_q)
        key = proj_ref[rows, GROUP * HS : (GROUP + 1) * HS]
        key = key * cosine + pltpu.roll(key, HS // 2, 1) * sine
        key = jnp.concatenate([key, pltpu.roll(key, HS // 2, 1)], axis=1).astype(jnp.bfloat16)
        value = proj_ref[rows, (GROUP + 1) * HS : (GROUP + 2) * HS].T.astype(jnp.bfloat16)
        value = jnp.concatenate([value, ones], axis=0)
        for g in range(GROUP):
            cols = slice(g * HS, (g + 1) * HS)
            query = proj_ref[rows, cols]
            query = jnp.concatenate([query * cosine, -(query * sine)], axis=1).astype(jnp.bfloat16)
            for low in range(0, RECLEN, QBLK):
                high = low + QBLK
                logits = lax.dot_general(
                    key[:high],
                    query[low:high],
                    (((1,), (1,)), ((), ())),
                    preferred_element_type=jnp.float32,
                )
                held = jnp.where(allowed[:high, low:high], logits, -1e30)
                top = jnp.max(held, axis=0, keepdims=True)
                weights = jnp.exp2((held - top) * scaling).astype(jnp.bfloat16)
                mixed = jnp.dot(value[:, :high], weights, preferred_element_type=jnp.float32)
                mixed = mixed[:HS] / mixed[HS : HS + 1]
                out_ref[rows.start + low : rows.start + high, cols] = mixed.T.astype(jnp.bfloat16)


def attend(normed, cosine, sine, segq, segk, pieces, after=()):
    vmem = pl.BlockSpec(memory_space=pltpu.VMEM)
    return pl.pallas_call(
        attend_kernel,
        out_shape=jax.ShapeDtypeStruct((2 * RECLEN, HEADS), jnp.bfloat16),
        in_specs=[vmem] * 15 + [pl.BlockSpec(memory_space=pl.ANY)] * len(after),
        out_specs=vmem,
        scratch_shapes=[pltpu.VMEM((2 * RECLEN, QKV), jnp.float32)],
        compiler_params=pltpu.CompilerParams(vmem_limit_bytes=ATTEND_VMEM),
        cost_estimate=pl.CostEstimate(
            flops=2 * 512 * WIDTH * QKV, bytes_accessed=16 << 20, transcendentals=1 << 20
        ),
        name="attend",
    )(normed, cosine, sine, segq, segk, *pieces, *after)


def arrange_kernel(head, offs_ref, line_ref, one_ref, three_ref, two_ref, out_ref, raw_ref, sems):
    copies = []
    for b, piece in enumerate((line_ref, one_ref, two_ref, three_ref)):
        for a in range(4):
            n = a * 4 + b
            row = a * BLK if b == 2 else (head * 4 + a) * BLK
            to = pl.multiple_of(offs_ref[n], BLK)
            copies.append(
                pltpu.make_async_copy(
                    piece.at[pl.ds(row, BLK)], raw_ref.at[pl.ds(to, BLK)], sems.at[n]
                )
            )
    for copy in copies:
        copy.start()
    for copy in copies:
        copy.wait()

    @pl.loop(0, 2 * COLS // 256)
    def _(n):
        rows = pl.ds(pl.multiple_of(n * 256, 256), 256)
        out_ref[:, rows] = raw_ref[rows, :].T


def arrange(offs, pieces, head):
    line, one, three, two_a, two_b = pieces
    return pl.pallas_call(
        lambda *refs: arrange_kernel(head, *refs),
        out_shape=jax.ShapeDtypeStruct((HEADS, 2 * COLS), jnp.bfloat16),
        in_specs=[pl.BlockSpec(memory_space=pltpu.SMEM)]
        + [pl.BlockSpec(memory_space=pl.ANY)] * 4,
        out_specs=pl.BlockSpec(memory_space=pltpu.VMEM),
        scratch_shapes=[
            pltpu.VMEM((2 * COLS, HEADS), jnp.bfloat16),
            pltpu.SemaphoreType.DMA((16,)),
        ],
        compiler_params=pltpu.CompilerParams(vmem_limit_bytes=SMALL_VMEM),
        cost_estimate=pl.CostEstimate(flops=0, bytes_accessed=8 << 20, transcendentals=0),
        name=f"arrange_{head}",
    )(offs, line, one, three, two_b if head else two_a)


def project_kernel(mixed_a_ref, mixed_b_ref, w_ref, meta_ref, weight_ref, *outs):
    score_ref = outs[-1]
    for part, out_ref in enumerate(outs[:2]):

        @pl.loop(0, COLS // 256)
        def _(n, part=part, out_ref=out_ref):
            from_cols = pl.ds(pl.multiple_of(part * COLS + n * 256, 256), 256)
            cols = pl.ds(pl.multiple_of(n * 256, 256), 256)
            for pair, mixed_ref in enumerate((mixed_a_ref, mixed_b_ref)):
                rows = slice(pair * 2 * RECLEN, (pair + 1) * 2 * RECLEN)
                out_ref[rows, cols] = jnp.dot(
                    mixed_ref[...], w_ref[:, from_cols], preferred_element_type=jnp.float32
                ).astype(jnp.bfloat16)

    scores = jnp.zeros((1, 128), jnp.float32)
    for i in range(4):
        rows = slice(i * RECLEN, (i + 1) * RECLEN)
        token = jnp.zeros((RECLEN, 1), jnp.float32)
        for part, out_ref in enumerate(outs[:2]):
            terms = out_ref[rows, :].astype(jnp.float32) * weight_ref[part : part + 1, :]
            token += jnp.sum(terms, axis=1, keepdims=True)
        scores += row_scores(token, meta_ref, i, 1)
    score_ref[...] = scores


def project(mixed_a, mixed_b, w, meta, weight):
    vmem = pl.BlockSpec(memory_space=pltpu.VMEM)
    return pl.pallas_call(
        project_kernel,
        out_shape=[jax.ShapeDtypeStruct((4 * RECLEN, COLS), jnp.bfloat16)] * 2
        + [jax.ShapeDtypeStruct((1, 128), jnp.float32)],
        in_specs=[vmem] * 3 + [pl.BlockSpec(memory_space=pltpu.SMEM), vmem],
        out_specs=[vmem] * 3,
        compiler_params=pltpu.CompilerParams(vmem_limit_bytes=PROJECT_VMEM),
        cost_estimate=pl.CostEstimate(
            flops=2 * 4 * RECLEN * HEADS * 2 * COLS, bytes_accessed=2 << 20, transcendentals=0
        ),
        name="project",
    )(mixed_a, mixed_b, w, meta, weight)


def row_scores(token, place_ref, first, count):
    slot = lax.broadcasted_iota(jnp.int32, (RECLEN, 1), 0)
    lane = lax.broadcasted_iota(jnp.int32, (1, 128), 1)
    scores = jnp.zeros((1, 128), jnp.float32)
    for i in range(count):
        row, length = place_ref[first + i], place_ref[8 + first + i]
        used = jnp.where(slot < length, token[i * RECLEN : (i + 1) * RECLEN], 0.0)
        scores += jnp.where(lane == row, jnp.sum(used, axis=0, keepdims=True), 0.0)
    return scores


def packed_rows(meta_ref, i, total):
    start, length = meta_ref[4 + i], meta_ref[8 + i]
    token = lax.broadcasted_iota(jnp.int32, (TOK, RECLEN), 0)
    slot = lax.broadcasted_iota(jnp.int32, (TOK, RECLEN), 1)
    pick = ((token - slot == start) & (slot < length)).astype(jnp.bfloat16)
    return jnp.dot(pick, total.astype(jnp.bfloat16), preferred_element_type=jnp.float32)


def finish_kernel(meta_ref, *refs):
    x_refs, kept_refs, in_refs = refs[:4], refs[4:6], refs[6:8]
    hidden_ref, acc_ref = refs[8:]
    for i in range(4):
        mine = slice(i * RECLEN, (i + 1) * RECLEN)
        theirs = slice((i ^ 1) * RECLEN, ((i ^ 1) + 1) * RECLEN)
        total = x_refs[i][...].astype(jnp.float32)
        for head in range(2):
            total += kept_refs[head][mine, :].astype(jnp.float32)
            total += in_refs[head][theirs, :].astype(jnp.float32)
        moved = packed_rows(meta_ref, i, total)
        if i == 0:
            acc_ref[...] = moved
        elif i < 3:
            acc_ref[...] += moved
        else:
            hidden_ref[...] = (acc_ref[...] + moved).astype(jnp.bfloat16)


def finish(meta, records, kept, swapped):
    def whole(shape):
        return pl.BlockSpec(shape, lambda i, m: (0,) * len(shape))

    slices = pl.BlockSpec((RECLEN, COLS), lambda i, m: (0, m[12]))
    return pl.pallas_call(
        finish_kernel,
        out_shape=jax.ShapeDtypeStruct((TOK, COLS), jnp.bfloat16),
        grid_spec=pltpu.PrefetchScalarGridSpec(
            num_scalar_prefetch=1,
            grid=(1,),
            in_specs=[slices] * 4 + [whole(v.shape) for v in (*kept, *swapped)],
            out_specs=whole((TOK, COLS)),
            scratch_shapes=[pltpu.VMEM((TOK, COLS), jnp.float32)],
        ),
        compiler_params=pltpu.CompilerParams(vmem_limit_bytes=FINISH_VMEM),
        cost_estimate=pl.CostEstimate(
            flops=2 * TOK * 4 * RECLEN * COLS, bytes_accessed=16 << 20, transcendentals=0
        ),
        name="finish",
    )(meta, *records, *kept, *swapped)


def record_score_kernel(meta_ref, record_ref, weight_ref, score_ref):
    token = jnp.sum(
        record_ref[...].astype(jnp.float32) * weight_ref[...], axis=1, keepdims=True
    )
    score_ref[...] = row_scores(token, meta_ref, 0, 1)


def record_score(meta, record, weight):
    vmem = pl.BlockSpec(memory_space=pltpu.VMEM)
    return pl.pallas_call(
        record_score_kernel,
        out_shape=jax.ShapeDtypeStruct((1, 128), jnp.float32),
        in_specs=[pl.BlockSpec(memory_space=pltpu.SMEM), vmem, vmem],
        out_specs=vmem,
        compiler_params=pltpu.CompilerParams(vmem_limit_bytes=SMALL_VMEM),
        cost_estimate=pl.CostEstimate(flops=2 << 20, bytes_accessed=2 << 20, transcendentals=0),
        name="record_score",
    )(meta, record, weight)


def on_device(records, lengths, assignment, segment_ids, norm_gain, w_qkv, w_out, score_weights):
    xh, co, xl, z, y = (lax.axis_index(a) for a in ("xh", "co", "xl", "z", "y"))
    row_index = xh * 2 + co
    reader_index = xl * 16 + z * 4 + y
    swap_xl, swap_xh, swap_co = ring("xl", 2, 1), ring("xh", 2, 1), ring("co", 2, 1)
    rec_ids = jnp.arange(32, dtype=jnp.int32)

    o_own = w_out.reshape(BLK, HEADS)
    here = xl == xh
    o_peer = swap_xl(o_own)
    o_across = lax.ppermute(o_own, ("xh", "xl"), [(0, 2), (2, 0), (1, 3), (3, 1)])
    o_corner = lax.ppermute(o_own, ("xh", "xl"), [(0, 3), (3, 0), (1, 2), (2, 1)])
    o_both = jnp.concatenate(
        [jnp.where(here, o_own, o_peer), jnp.where(here, o_across, o_corner)], axis=0
    )

    w_own = w_qkv.reshape(BLK, QKV)
    w_peer = swap_xl(w_own)
    own_line = plane_gather_first(w_own, 1)

    own_assign = lax.dynamic_index_in_dim(assignment, row_index, 0, keepdims=False)
    outgoing = jnp.sum(
        jnp.where(own_assign[None, :] == rec_ids[:, None], rec_ids[None, :], 0), axis=1
    )
    send_block = order_records(outgoing, records.reshape(32, 8, WIDTH), [o_both, own_line, w_peer])
    arrived = lax.all_to_all(
        send_block, ("xl", "z", "y"), split_axis=0, concat_axis=0, tiled=True
    )
    own_record = arrived.reshape(RECLEN, WIDTH)
    peer_record = swap_co(own_record)

    own_pieces = plane_gather_second(stack([own_line], [(0, 0, 4 * BLK)], own_record))
    peer_pieces = plane_gather_second(
        plane_gather_first(stack([w_peer], [(0, 0, BLK)], own_record), 1)
    )
    qkv_pieces = own_pieces + peer_pieces
    o_both = stack([o_both], [(0, 0, 2 * BLK)], peer_pieces[3:] + own_pieces[3:])
    out_pieces = plane_gather_second(plane_gather_first(o_both, 2))

    far_record = stack([swap_xh(own_record)], [(0, 0, RECLEN)], peer_pieces[1:3])
    far_peer_record = swap_co(far_record)
    slots = [own_record, peer_record, far_record, far_peer_record]

    chosen = assignment == reader_index
    row_order = jnp.stack(
        [row_index, row_index + 1 - 2 * co, row_index + 2 - 4 * xh, 3 - row_index]
    )
    pick_row = row_order[:, None] == jnp.arange(4, dtype=jnp.int32)[None, :]
    lens = jnp.sum(jnp.where(chosen, lengths, 0), axis=1)
    segs = jnp.sum(jnp.where(chosen[:, :, None], segment_ids, 0), axis=1)
    local_lens = jnp.sum(jnp.where(pick_row, lens[None, :], 0), axis=1)
    before = jnp.arange(4, dtype=jnp.int32)[None, :] < row_order[:, None]
    local_starts = jnp.sum(jnp.where(before, lens[None, :], 0), axis=1)
    local_segs = jnp.sum(jnp.where(pick_row[:, :, None], segs[None], 0), axis=1)
    segq = local_segs[:, :, None]
    segk = local_segs[:, None, :]
    meta = jnp.concatenate([row_order, local_starts, local_lens, row_index[None]])

    inv_freq = ROPE_BASE ** (-(jnp.arange(HS // 2, dtype=jnp.float32) * 2.0 / HS))
    angle = jnp.arange(RECLEN, dtype=jnp.float32)[:, None] * inv_freq[None, :]
    cosine = jnp.cos(angle)
    sine = jnp.sin(angle)
    cosine = jnp.concatenate([cosine, cosine], axis=1)
    sine = jnp.concatenate([-sine, sine], axis=1)


    steps_a = jnp.arange(4, dtype=jnp.int32)[:, None]
    steps_b = jnp.arange(4, dtype=jnp.int32)[None, :]
    src_z = jnp.where(co == 0, z - steps_b, z - steps_a) & 3
    src_y = jnp.where(co == 0, y - steps_a, y - steps_b) & 3
    plane = BLK * (src_z * 4 + src_y)
    plane = jnp.stack([plane[:, b] for b in (0, 1, 3, 2)]).reshape(16)
    qkv_offs = jnp.concatenate([xl * 2048 + plane, (1 - xl) * 2048 + plane])
    kept = ((src_z // 2) == co).astype(jnp.int32)
    out_offs = (kept * COLS + (src_z & 1) * (4 * BLK) + src_y * BLK).reshape(16)

    gain = norm_gain[None, :]
    normed_a = normalize(qkv_offs, slots[0], slots[1], gain)
    normed_b = normalize(qkv_offs, slots[2], slots[3], gain)
    mixed_a = attend(normed_a, cosine, sine, segq[:2], segk[:2], qkv_pieces, [normed_b])
    mixed_b = attend(normed_b, cosine, sine, segq[2:], segk[2:], qkv_pieces)
    far_b = swap_xh(mixed_a)
    far_a = swap_xh(mixed_b)
    weights = score_weights.reshape(4, COLS)
    weight = jnp.stack(
        [
            lax.dynamic_index_in_dim(weights, row_index + 1 - 2 * co, 0, keepdims=False),
            lax.dynamic_index_in_dim(weights, row_index, 0, keepdims=False),
        ]
    )
    w_near, w_far = arrange(out_offs, out_pieces, 0), arrange(out_offs, out_pieces, 1)

    terms = [
        project(mixed_a, mixed_b, w_near, meta, weight),
        project(far_a, far_b, w_far, meta, weight),
    ]
    hidden_out = finish(meta, slots, [t[1] for t in terms], [swap_co(t[0]) for t in terms])
    scores = record_score(meta, own_record, score_weights[None, :])
    scores += terms[0][2] + terms[1][2]
    scores += swap_co(scores)
    scores += stack([swap_xh(scores)], [(0, 0, 1)], hidden_out)
    scores = scores[0, :4]
    record_scores = (scores / lens.astype(jnp.float32))[None, :]
    return (hidden_out, record_scores)


def solution(mesh):
    fine = Mesh(mesh.devices.reshape(2, 2, 2, 4, 4), ("xh", "co", "xl", "z", "y"))
    row, reader = ("xh", "co"), ("xl", "z", "y")
    in_specs = (
        P(row, None, reader, None),
        P(),
        P(),
        P(),
        P(),
        P(reader, row, None),
        P(reader, row, None),
        P(),
    )
    out_specs = (P(reader, row), P(reader, None))
    return jax.shard_map(
        on_device, mesh=fine, in_specs=in_specs, out_specs=out_specs, check_vma=False
    )
```

```python
import math

import jax
import jax.numpy as jnp
from jax import lax
from jax.experimental import pallas as pl
from jax.experimental.pallas import tpu as pltpu
from jax.sharding import Mesh, PartitionSpec as P

HS = 128
GROUP = 8
RECLEN = 256
WIDTH = 4096
TOK = 896
QKV = (GROUP + 2) * HS
HEADS = GROUP * HS
COLS = WIDTH // 4
ROPE_BASE = 500000.0
BLK = 128
QBLK = 256
ATTEND_VMEM = 16 << 20
SMALL_VMEM = 12 << 20
PROJECT_VMEM = 16 << 20
FINISH_VMEM = 28 << 20

CORE_ZY = ("co", "z", "y")


def ring(axis, size, step):
    return lambda v: lax.ppermute(v, axis, [(i, (i + step) % size) for i in range(size)])


def plane_perm(step, first):
    pairs = []
    for co in range(2):
        for z in range(4):
            for y in range(4):
                along_y = (co == 0) == first
                z2, y2 = (z, (y + step) % 4) if along_y else ((z + step) % 4, y)
                pairs.append((co * 16 + z * 4 + y, co * 16 + z2 * 4 + y2))
    return lambda v: lax.ppermute(v, CORE_ZY, pairs)


def stack_kernel(plan, *refs):
    out_ref = refs[-1]
    to = 0
    for which, row, rows in plan:
        out_ref[to : to + rows] = refs[which][row : row + rows]
        to += rows


def stack(arrays, plan, after=None):
    rows = sum(p[2] for p in plan)
    held = [] if after is None else after if isinstance(after, list) else [after]
    return pl.pallas_call(
        lambda *refs: stack_kernel(plan, *refs),
        out_shape=jax.ShapeDtypeStruct((rows, arrays[0].shape[1]), arrays[0].dtype),
        in_specs=[pl.BlockSpec(memory_space=pltpu.VMEM)] * len(arrays)
        + [pl.BlockSpec(memory_space=pl.ANY)] * len(held),
        out_specs=pl.BlockSpec(memory_space=pltpu.VMEM),
        compiler_params=pltpu.CompilerParams(vmem_limit_bytes=SMALL_VMEM),
        cost_estimate=pl.CostEstimate(flops=0, bytes_accessed=1 << 20, transcendentals=0),
        name="stack",
    )(*arrays, *held)


def plane_gather_first(block, groups, after=None):
    one = plane_perm(1, True)(block)
    three = plane_perm(-1, True)(block)
    two = plane_perm(2, True)(block)
    plan = [(i, g * BLK, BLK) for g in range(groups) for i in range(4)]
    return stack([block, one, two, three], plan, after)


def plane_gather_second(line):
    half = line.shape[0] // 2
    one = plane_perm(1, False)(line)
    three = plane_perm(-1, False)(line)
    two_a = plane_perm(1, False)(one[:half])
    two_b = plane_perm(-1, False)(three[half:])
    return [line, one, three, two_a, two_b]


def order_kernel(outgoing_ref, records_ref, *rest):
    out_ref, sems = rest[-2:]
    copies = [
        pltpu.make_async_copy(records_ref.at[outgoing_ref[j]], out_ref.at[j], sems.at[j])
        for j in range(32)
    ]
    for copy in copies:
        copy.start()
    for copy in copies:
        copy.wait()


def order_records(outgoing, records, after):
    return pl.pallas_call(
        order_kernel,
        out_shape=jax.ShapeDtypeStruct(records.shape, records.dtype),
        in_specs=[pl.BlockSpec(memory_space=pltpu.SMEM)]
        + [pl.BlockSpec(memory_space=pl.ANY)] * (1 + len(after)),
        out_specs=pl.BlockSpec(memory_space=pltpu.VMEM),
        scratch_shapes=[pltpu.SemaphoreType.DMA((32,))],
        cost_estimate=pl.CostEstimate(flops=0, bytes_accessed=4 << 20, transcendentals=0),
        name="order_records",
    )(outgoing, records, *after)


def normalize_kernel(offs_ref, xa_ref, xb_ref, gain_ref, normed_ref):
    for part, x_ref in enumerate((xa_ref, xb_ref)):

        @pl.loop(0, RECLEN // 32)
        def _(i, part=part, x_ref=x_ref):
            rows = pl.ds(pl.multiple_of(i * 32, 32), 32)
            into = pl.ds(pl.multiple_of(part * RECLEN + i * 32, 32), 32)
            x = x_ref[rows, :].astype(jnp.float32)
            scale = lax.rsqrt(jnp.mean(x * x, axis=1, keepdims=True) + 1e-05)
            for n in range(32):
                cols = pl.ds(pl.multiple_of(offs_ref[n], BLK), BLK)
                normed_ref[into, n * BLK : (n + 1) * BLK] = (
                    x_ref[rows, cols].astype(jnp.float32) * scale * gain_ref[:, cols]
                ).astype(jnp.bfloat16)


def normalize(offs, xa, xb, gain):
    vmem = pl.BlockSpec(memory_space=pltpu.VMEM)
    return pl.pallas_call(
        normalize_kernel,
        out_shape=jax.ShapeDtypeStruct((2 * RECLEN, WIDTH), jnp.bfloat16),
        in_specs=[pl.BlockSpec(memory_space=pltpu.SMEM)] + [vmem] * 3,
        out_specs=vmem,
        compiler_params=pltpu.CompilerParams(vmem_limit_bytes=SMALL_VMEM),
        cost_estimate=pl.CostEstimate(
            flops=2 * 512 * WIDTH, bytes_accessed=12 << 20, transcendentals=0
        ),
        name="normalize",
    )(offs, xa, xb, gain)


def attend_kernel(normed_ref, cos_ref, sin_ref, segq_ref, segk_ref, *rest):
    pieces = rest[:10]
    out_ref, proj_ref = rest[-2:]

    @pl.loop(0, QKV // 256)
    def _(n):
        cols = pl.ds(pl.multiple_of(n * 256, 256), 256)
        total, start = 0.0, 0
        for piece in pieces:
            stop = start + piece.shape[0]
            total += jnp.dot(
                normed_ref[:, start:stop], piece[:, cols], preferred_element_type=jnp.float32
            )
            start = stop
        proj_ref[:, cols] = total

    cosine = cos_ref[...]
    sine = sin_ref[...]
    place_k = lax.broadcasted_iota(jnp.int32, (RECLEN, RECLEN), 0)
    place_q = lax.broadcasted_iota(jnp.int32, (RECLEN, RECLEN), 1)
    scaling = math.log2(math.e) / math.sqrt(HS)
    ones = jnp.ones((16, RECLEN), jnp.bfloat16)
    for part in range(2):
        rows = slice(part * RECLEN, (part + 1) * RECLEN)
        allowed = (segq_ref[part] == segk_ref[part]) & (place_k <= place_q)
        key = proj_ref[rows, GROUP * HS : (GROUP + 1) * HS]
        key = key * cosine + pltpu.roll(key, HS // 2, 1) * sine
        key = jnp.concatenate([key, pltpu.roll(key, HS // 2, 1)], axis=1).astype(jnp.bfloat16)
        value = proj_ref[rows, (GROUP + 1) * HS : (GROUP + 2) * HS].T.astype(jnp.bfloat16)
        value = jnp.concatenate([value, ones], axis=0)
        for g in range(GROUP):
            cols = slice(g * HS, (g + 1) * HS)
            query = proj_ref[rows, cols]
            query = jnp.concatenate([query * cosine, -(query * sine)], axis=1).astype(jnp.bfloat16)
            for low in range(0, RECLEN, QBLK):
                high = low + QBLK
                logits = lax.dot_general(
                    key[:high],
                    query[low:high],
                    (((1,), (1,)), ((), ())),
                    preferred_element_type=jnp.float32,
                )
                held = jnp.where(allowed[:high, low:high], logits, -1e30)
                top = jnp.max(held, axis=0, keepdims=True)
                weights = jnp.exp2((held - top) * scaling).astype(jnp.bfloat16)
                mixed = jnp.dot(value[:, :high], weights, preferred_element_type=jnp.float32)
                mixed = mixed[:HS] / mixed[HS : HS + 1]
                out_ref[rows.start + low : rows.start + high, cols] = mixed.T.astype(jnp.bfloat16)


def attend(normed, cosine, sine, segq, segk, pieces, after=()):
    vmem = pl.BlockSpec(memory_space=pltpu.VMEM)
    return pl.pallas_call(
        attend_kernel,
        out_shape=jax.ShapeDtypeStruct((2 * RECLEN, HEADS), jnp.bfloat16),
        in_specs=[vmem] * 15 + [pl.BlockSpec(memory_space=pl.ANY)] * len(after),
        out_specs=vmem,
        scratch_shapes=[pltpu.VMEM((2 * RECLEN, QKV), jnp.float32)],
        compiler_params=pltpu.CompilerParams(vmem_limit_bytes=ATTEND_VMEM),
        cost_estimate=pl.CostEstimate(
            flops=2 * 512 * WIDTH * QKV, bytes_accessed=16 << 20, transcendentals=1 << 20
        ),
        name="attend",
    )(normed, cosine, sine, segq, segk, *pieces, *after)


def arrange_kernel(head, offs_ref, line_ref, one_ref, three_ref, two_ref, out_ref, raw_ref, sems):
    copies = []
    for b, piece in enumerate((line_ref, one_ref, two_ref, three_ref)):
        for a in range(4):
            n = a * 4 + b
            row = a * BLK if b == 2 else (head * 4 + a) * BLK
            to = pl.multiple_of(offs_ref[n], BLK)
            copies.append(
                pltpu.make_async_copy(
                    piece.at[pl.ds(row, BLK)], raw_ref.at[pl.ds(to, BLK)], sems.at[n]
                )
            )
    for copy in copies:
        copy.start()
    for copy in copies:
        copy.wait()

    @pl.loop(0, 2 * COLS // 256)
    def _(n):
        rows = pl.ds(pl.multiple_of(n * 256, 256), 256)
        out_ref[:, rows] = raw_ref[rows, :].T


def arrange(offs, pieces, head):
    line, one, three, two_a, two_b = pieces
    return pl.pallas_call(
        lambda *refs: arrange_kernel(head, *refs),
        out_shape=jax.ShapeDtypeStruct((HEADS, 2 * COLS), jnp.bfloat16),
        in_specs=[pl.BlockSpec(memory_space=pltpu.SMEM)]
        + [pl.BlockSpec(memory_space=pl.ANY)] * 4,
        out_specs=pl.BlockSpec(memory_space=pltpu.VMEM),
        scratch_shapes=[
            pltpu.VMEM((2 * COLS, HEADS), jnp.bfloat16),
            pltpu.SemaphoreType.DMA((16,)),
        ],
        compiler_params=pltpu.CompilerParams(vmem_limit_bytes=SMALL_VMEM),
        cost_estimate=pl.CostEstimate(flops=0, bytes_accessed=8 << 20, transcendentals=0),
        name=f"arrange_{head}",
    )(offs, line, one, three, two_b if head else two_a)


def project_kernel(mixed_a_ref, mixed_b_ref, w_ref, meta_ref, weight_ref, *outs):
    score_ref = outs[-1]
    for part, out_ref in enumerate(outs[:2]):

        @pl.loop(0, COLS // 256)
        def _(n, part=part, out_ref=out_ref):
            from_cols = pl.ds(pl.multiple_of(part * COLS + n * 256, 256), 256)
            cols = pl.ds(pl.multiple_of(n * 256, 256), 256)
            for pair, mixed_ref in enumerate((mixed_a_ref, mixed_b_ref)):
                rows = slice(pair * 2 * RECLEN, (pair + 1) * 2 * RECLEN)
                out_ref[rows, cols] = jnp.dot(
                    mixed_ref[...], w_ref[:, from_cols], preferred_element_type=jnp.float32
                ).astype(jnp.bfloat16)

    scores = jnp.zeros((1, 128), jnp.float32)
    for i in range(4):
        rows = slice(i * RECLEN, (i + 1) * RECLEN)
        token = jnp.zeros((RECLEN, 1), jnp.float32)
        for part, out_ref in enumerate(outs[:2]):
            terms = out_ref[rows, :].astype(jnp.float32) * weight_ref[part : part + 1, :]
            token += jnp.sum(terms, axis=1, keepdims=True)
        scores += row_scores(token, meta_ref, i, 1)
    score_ref[...] = scores


def project(mixed_a, mixed_b, w, meta, weight):
    vmem = pl.BlockSpec(memory_space=pltpu.VMEM)
    return pl.pallas_call(
        project_kernel,
        out_shape=[jax.ShapeDtypeStruct((4 * RECLEN, COLS), jnp.bfloat16)] * 2
        + [jax.ShapeDtypeStruct((1, 128), jnp.float32)],
        in_specs=[vmem] * 3 + [pl.BlockSpec(memory_space=pltpu.SMEM), vmem],
        out_specs=[vmem] * 3,
        compiler_params=pltpu.CompilerParams(vmem_limit_bytes=PROJECT_VMEM),
        cost_estimate=pl.CostEstimate(
            flops=2 * 4 * RECLEN * HEADS * 2 * COLS, bytes_accessed=2 << 20, transcendentals=0
        ),
        name="project",
    )(mixed_a, mixed_b, w, meta, weight)


def row_scores(token, place_ref, first, count):
    slot = lax.broadcasted_iota(jnp.int32, (RECLEN, 1), 0)
    lane = lax.broadcasted_iota(jnp.int32, (1, 128), 1)
    scores = jnp.zeros((1, 128), jnp.float32)
    for i in range(count):
        row, length = place_ref[first + i], place_ref[8 + first + i]
        used = jnp.where(slot < length, token[i * RECLEN : (i + 1) * RECLEN], 0.0)
        scores += jnp.where(lane == row, jnp.sum(used, axis=0, keepdims=True), 0.0)
    return scores


def packed_rows(meta_ref, i, total):
    start, length = meta_ref[4 + i], meta_ref[8 + i]
    token = lax.broadcasted_iota(jnp.int32, (TOK, RECLEN), 0)
    slot = lax.broadcasted_iota(jnp.int32, (TOK, RECLEN), 1)
    pick = ((token - slot == start) & (slot < length)).astype(jnp.bfloat16)
    return jnp.dot(pick, total.astype(jnp.bfloat16), preferred_element_type=jnp.float32)


def finish_kernel(meta_ref, *refs):
    x_refs, kept_refs, in_refs = refs[:4], refs[4:6], refs[6:8]
    hidden_ref, acc_ref = refs[8:]
    for i in range(4):
        mine = slice(i * RECLEN, (i + 1) * RECLEN)
        theirs = slice((i ^ 1) * RECLEN, ((i ^ 1) + 1) * RECLEN)
        total = x_refs[i][...].astype(jnp.float32)
        for head in range(2):
            total += kept_refs[head][mine, :].astype(jnp.float32)
            total += in_refs[head][theirs, :].astype(jnp.float32)
        moved = packed_rows(meta_ref, i, total)
        if i == 0:
            acc_ref[...] = moved
        elif i < 3:
            acc_ref[...] += moved
        else:
            hidden_ref[...] = (acc_ref[...] + moved).astype(jnp.bfloat16)


def finish(meta, records, kept, swapped):
    def whole(shape):
        return pl.BlockSpec(shape, lambda i, m: (0,) * len(shape))

    slices = pl.BlockSpec((RECLEN, COLS), lambda i, m: (0, m[12]))
    return pl.pallas_call(
        finish_kernel,
        out_shape=jax.ShapeDtypeStruct((TOK, COLS), jnp.bfloat16),
        grid_spec=pltpu.PrefetchScalarGridSpec(
            num_scalar_prefetch=1,
            grid=(1,),
            in_specs=[slices] * 4 + [whole(v.shape) for v in (*kept, *swapped)],
            out_specs=whole((TOK, COLS)),
            scratch_shapes=[pltpu.VMEM((TOK, COLS), jnp.float32)],
        ),
        compiler_params=pltpu.CompilerParams(vmem_limit_bytes=FINISH_VMEM),
        cost_estimate=pl.CostEstimate(
            flops=2 * TOK * 4 * RECLEN * COLS, bytes_accessed=16 << 20, transcendentals=0
        ),
        name="finish",
    )(meta, *records, *kept, *swapped)


def record_score_kernel(meta_ref, record_ref, weight_ref, score_ref):
    token = jnp.sum(
        record_ref[...].astype(jnp.float32) * weight_ref[...], axis=1, keepdims=True
    )
    score_ref[...] = row_scores(token, meta_ref, 0, 1)


def record_score(meta, record, weight):
    vmem = pl.BlockSpec(memory_space=pltpu.VMEM)
    return pl.pallas_call(
        record_score_kernel,
        out_shape=jax.ShapeDtypeStruct((1, 128), jnp.float32),
        in_specs=[pl.BlockSpec(memory_space=pltpu.SMEM), vmem, vmem],
        out_specs=vmem,
        compiler_params=pltpu.CompilerParams(vmem_limit_bytes=SMALL_VMEM),
        cost_estimate=pl.CostEstimate(flops=2 << 20, bytes_accessed=2 << 20, transcendentals=0),
        name="record_score",
    )(meta, record, weight)


def on_device(records, lengths, assignment, segment_ids, norm_gain, w_qkv, w_out, score_weights):
    xh, co, xl, z, y = (lax.axis_index(a) for a in ("xh", "co", "xl", "z", "y"))
    row_index = xh * 2 + co
    reader_index = xl * 16 + z * 4 + y
    swap_xl, swap_xh, swap_co = ring("xl", 2, 1), ring("xh", 2, 1), ring("co", 2, 1)
    rec_ids = jnp.arange(32, dtype=jnp.int32)

    o_own = w_out.reshape(BLK, HEADS)
    here = xl == xh
    o_peer = swap_xl(o_own)
    o_across = lax.ppermute(o_own, ("xh", "xl"), [(0, 2), (2, 0), (1, 3), (3, 1)])
    o_corner = lax.ppermute(o_own, ("xh", "xl"), [(0, 3), (3, 0), (1, 2), (2, 1)])
    o_both = jnp.concatenate(
        [jnp.where(here, o_own, o_peer), jnp.where(here, o_across, o_corner)], axis=0
    )

    w_own = w_qkv.reshape(BLK, QKV)
    w_peer = swap_xl(w_own)
    own_line = plane_gather_first(w_own, 1)

    own_assign = lax.dynamic_index_in_dim(assignment, row_index, 0, keepdims=False)
    outgoing = jnp.sum(
        jnp.where(own_assign[None, :] == rec_ids[:, None], rec_ids[None, :], 0), axis=1
    )
    send_block = order_records(outgoing, records.reshape(32, 8, WIDTH), [o_both, own_line, w_peer])
    arrived = lax.all_to_all(
        send_block, ("xl", "z", "y"), split_axis=0, concat_axis=0, tiled=True
    )
    own_record = arrived.reshape(RECLEN, WIDTH)
    peer_record = swap_co(own_record)

    own_pieces = plane_gather_second(stack([own_line], [(0, 0, 4 * BLK)], own_record))
    peer_pieces = plane_gather_second(
        plane_gather_first(stack([w_peer], [(0, 0, BLK)], own_record), 1)
    )
    qkv_pieces = own_pieces + peer_pieces

    far_record = stack([swap_xh(own_record)], [(0, 0, RECLEN)], peer_pieces[1:3])
    far_peer_record = swap_co(far_record)
    slots = [own_record, peer_record, far_record, far_peer_record]

    chosen = assignment == reader_index
    row_order = jnp.stack(
        [row_index, row_index + 1 - 2 * co, row_index + 2 - 4 * xh, 3 - row_index]
    )
    pick_row = row_order[:, None] == jnp.arange(4, dtype=jnp.int32)[None, :]
    lens = jnp.sum(jnp.where(chosen, lengths, 0), axis=1)
    segs = jnp.sum(jnp.where(chosen[:, :, None], segment_ids, 0), axis=1)
    local_lens = jnp.sum(jnp.where(pick_row, lens[None, :], 0), axis=1)
    before = jnp.arange(4, dtype=jnp.int32)[None, :] < row_order[:, None]
    local_starts = jnp.sum(jnp.where(before, lens[None, :], 0), axis=1)
    local_segs = jnp.sum(jnp.where(pick_row[:, :, None], segs[None], 0), axis=1)
    segq = local_segs[:, :, None]
    segk = local_segs[:, None, :]
    meta = jnp.concatenate([row_order, local_starts, local_lens, row_index[None]])

    inv_freq = ROPE_BASE ** (-(jnp.arange(HS // 2, dtype=jnp.float32) * 2.0 / HS))
    angle = jnp.arange(RECLEN, dtype=jnp.float32)[:, None] * inv_freq[None, :]
    cosine = jnp.cos(angle)
    sine = jnp.sin(angle)
    cosine = jnp.concatenate([cosine, cosine], axis=1)
    sine = jnp.concatenate([-sine, sine], axis=1)


    steps_a = jnp.arange(4, dtype=jnp.int32)[:, None]
    steps_b = jnp.arange(4, dtype=jnp.int32)[None, :]
    src_z = jnp.where(co == 0, z - steps_b, z - steps_a) & 3
    src_y = jnp.where(co == 0, y - steps_a, y - steps_b) & 3
    plane = BLK * (src_z * 4 + src_y)
    plane = jnp.stack([plane[:, b] for b in (0, 1, 3, 2)]).reshape(16)
    qkv_offs = jnp.concatenate([xl * 2048 + plane, (1 - xl) * 2048 + plane])
    kept = ((src_z // 2) == co).astype(jnp.int32)
    out_offs = (kept * COLS + (src_z & 1) * (4 * BLK) + src_y * BLK).reshape(16)

    gain = norm_gain[None, :]
    normed_a = normalize(qkv_offs, slots[0], slots[1], gain)
    normed_b = normalize(qkv_offs, slots[2], slots[3], gain)
    o_both = stack([o_both], [(0, 0, 2 * BLK)], peer_pieces[3:] + own_pieces[3:] + [normed_a])
    out_pieces = plane_gather_second(plane_gather_first(o_both, 2))
    mixed_a = attend(normed_a, cosine, sine, segq[:2], segk[:2], qkv_pieces, [normed_b])
    mixed_b = attend(normed_b, cosine, sine, segq[2:], segk[2:], qkv_pieces)
    far_b = swap_xh(mixed_a)
    far_a = swap_xh(mixed_b)
    weights = score_weights.reshape(4, COLS)
    weight = jnp.stack(
        [
            lax.dynamic_index_in_dim(weights, row_index + 1 - 2 * co, 0, keepdims=False),
            lax.dynamic_index_in_dim(weights, row_index, 0, keepdims=False),
        ]
    )
    w_near, w_far = arrange(out_offs, out_pieces, 0), arrange(out_offs, out_pieces, 1)

    terms = [
        project(mixed_a, mixed_b, w_near, meta, weight),
        project(far_a, far_b, w_far, meta, weight),
    ]
    hidden_out = finish(meta, slots, [t[1] for t in terms], [swap_co(t[0]) for t in terms])
    scores = record_score(meta, own_record, score_weights[None, :])
    scores += terms[0][2] + terms[1][2]
    scores += swap_co(scores)
    scores += stack([swap_xh(scores)], [(0, 0, 1)], hidden_out)
    scores = scores[0, :4]
    record_scores = (scores / lens.astype(jnp.float32))[None, :]
    return (hidden_out, record_scores)


def solution(mesh):
    fine = Mesh(mesh.devices.reshape(2, 2, 2, 4, 4), ("xh", "co", "xl", "z", "y"))
    row, reader = ("xh", "co"), ("xl", "z", "y")
    in_specs = (
        P(row, None, reader, None),
        P(),
        P(),
        P(),
        P(),
        P(reader, row, None),
        P(reader, row, None),
        P(),
    )
    out_specs = (P(reader, row), P(reader, None))
    return jax.shard_map(
        on_device, mesh=fine, in_specs=in_specs, out_specs=out_specs, check_vma=False
    )
```
